256 devices in a mesh: lat: 8 (over y_lo, x), lon: 32 (over z, y_hi, core).
Axes of the slice: x: 4, y: 4 (y_hi: 2, y_lo: 2; y = y_hi * 2 + y_lo), z: 8, core: 2. Of those that a mesh axis runs over, the one named last changes fastest.
Arguments:
- signal: bfloat16 [64, 196608], P('lat', 'lon'), may hold values from -6 to 6
- cotangent: bfloat16 [64, 196608], P('lat', 'lon'), may hold values from -6 to 6
- qkv_weight: bfloat16 [2, 96, 288], replicated, may hold values from -0.625 to 0.625
- proj_weight: bfloat16 [2, 96, 96], replicated, may hold values from -0.625 to 0.625
- up_weight: bfloat16 [2, 96, 384], replicated, may hold values from -0.625 to 0.625
- down_weight: bfloat16 [2, 384, 96], replicated, may hold values from -0.3125 to 0.3125
- gdn_gamma: float32 [2, 96, 96], replicated, may hold values from 0.001 to 0.02
- gdn_beta: float32 [2, 96], replicated, may hold values from 0.25 to 4
- rel_table: float32 [2, 3, 225], replicated, may hold values from -3 to 250
Outputs:
- decoded: bfloat16 [64, 196608], P('lat', 'lon')
- signal_grad: bfloat16 [64, 196608], P('lat', 'lon')
- qkv_grad: float32 [2, 96, 288], replicated
- proj_grad: float32 [2, 96, 96], replicated
- up_grad: float32 [2, 96, 384], replicated
- down_grad: float32 [2, 384, 96], replicated
- gamma_grad: float32 [2, 96, 96], replicated
- beta_grad: float32 [2, 96], replicated
- table_grad: float32 [2, 3, 225], replicated
The draws below stay inside these ranges and needn't reach their ends.
All inputs are finite; a program needn't handle non-finite values.
Results may differ from the reference program's by a relative error of at most 0.025.
Values may be sent and summed in bfloat16 or wider, within the bound.
A program may use at most 64 MiB of HBM per device.

```python
import math
import jax
import jax.numpy as jnp
from jax import lax

C = 96
HEADS = 3
HID = 384
WIN = 8
SHIFT = 4
RELS = 225
H_DEV = 8
W_DEV = 64
NLAT = 64
NLON = 2048
PIXELS = 131072
N_LAT = 8
N_LON = 32


def draw_rel_table(key, part):
    key = jax.random.fold_in(key, 7)
    key_base = jax.random.fold_in(key, 0)
    return jnp.clip(jax.random.normal(key_base, (2, HEADS, RELS), jnp.float32) * 1.5, -3.0, 3.0)


def levels(own_key, extent, cuts, least, top_value):
    def one(dim, shards_of):
        draws = jax.random.uniform(jax.random.fold_in(jax.random.fold_in(own_key, 6), dim), (shards_of,), jnp.float32, least / len(cuts), top_value / len(cuts))
        return jnp.repeat(jnp.exp(draws), extent[dim] // shards_of).reshape((-1,) + (1,) * (len(extent) - dim - 1))

    factor_of = one(*cuts[0])
    for cut in cuts[1:]:
        factor_of = factor_of * one(*cut)
    return factor_of


def bell_draw(own_key, shape, scale, limit, cuts=(), kind=jnp.bfloat16):
    array = jax.random.normal(own_key, shape, jnp.float32) * scale
    if len(cuts) > 0:
        array = levels(own_key, shape, cuts, -0.22, 0.18) * array
    return jnp.clip(array, min=-limit, max=limit).astype(kind)


def setup_inputs(seed: int = 0) -> dict:
    arg_keys = jax.random.split(jax.random.key(seed), 10)
    signal = bell_draw(arg_keys[0], (NLAT, NLON * C), 1.0, 6.0, ((0, 8), (1, 32)))
    cotangent = bell_draw(arg_keys[1], (NLAT, NLON * C), 1.0, 6.0, ((0, 8), (1, 32)))
    qkv_weight = bell_draw(arg_keys[2], (2, C, 3 * C), C ** -0.5, 0.625)
    proj_weight = bell_draw(arg_keys[3], (2, C, C), C ** -0.5, 0.625)
    up_weight = bell_draw(arg_keys[4], (2, C, HID), C ** -0.5, 0.625)
    down_weight = bell_draw(arg_keys[5], (2, HID, C), HID ** -0.5, 0.3125)
    gdn_gamma = jnp.clip(jax.random.uniform(arg_keys[6], (2, C, C), jnp.float32, 0.001, 0.02), 0.001, 0.02)
    gdn_beta = jnp.clip(jnp.exp(jax.random.uniform(arg_keys[7], (2, C), jnp.float32, math.log(0.25), math.log(4.0))), 0.25, 4.0)
    rel_table = draw_rel_table(jax.random.fold_in(arg_keys[9], 71), 0)
    return {"signal": signal, "cotangent": cotangent, "qkv_weight": qkv_weight, "proj_weight": proj_weight, "up_weight": up_weight, "down_weight": down_weight, "gdn_gamma": gdn_gamma, "gdn_beta": gdn_beta, "rel_table": rel_table}


def layer_normed(values_in):
    center = values_in - lax.optimization_barrier(jnp.mean(values_in, axis=-1, keepdims=True))
    spread = lax.optimization_barrier(jnp.mean(center * center, axis=-1, keepdims=True))
    return center * lax.rsqrt(spread + 1e-05)

def offset_table():
    places = jnp.arange(WIN * WIN, dtype=jnp.int32)
    across = places // WIN
    inside = places % WIN
    offset = (across[:, None] - across[None, :] + WIN - 1) * (2 * WIN - 1) + (inside[:, None] - inside[None, :] + WIN - 1)
    slot_ids = jnp.arange((2 * WIN - 1) ** 2, dtype=jnp.int32)
    return (offset.reshape(-1)[:, None] == slot_ids[None, :]).astype(jnp.float32)

def to_windows(grid_data):
    rows_in, cols_in, channels = grid_data.shape
    grid_data = grid_data.reshape(rows_in // WIN, WIN, cols_in // WIN, WIN, channels)
    return grid_data.transpose(0, 2, 1, 3, 4).reshape(-1, WIN * WIN, channels)

def from_windows(grid_data, rows_in, cols_in):
    channels = grid_data.shape[-1]
    grid_data = grid_data.reshape(rows_in // WIN, cols_in // WIN, WIN, WIN, channels)
    return grid_data.transpose(0, 2, 1, 3, 4).reshape(rows_in, cols_in, channels)

def swin_block(tile_in, params, region):
    qkv_weight, proj_weight, up_weight, down_weight, gdn_gamma, gdn_beta, rel_table = params
    rows_in, cols_in = (tile_in.shape[0], tile_in.shape[1])
    head_size = C // HEADS
    signal = tile_in.astype(jnp.float32)
    normed = to_windows(layer_normed(signal).astype(jnp.bfloat16)).reshape(-1, C)
    triple = jnp.dot(normed, qkv_weight, preferred_element_type=jnp.float32).astype(jnp.bfloat16)
    triple = triple.reshape(-1, WIN * WIN, 3, HEADS, head_size)
    scores = jnp.einsum('nqhd,nkhd->nhqk', triple[:, :, 0].astype(jnp.float32), triple[:, :, 1].astype(jnp.float32))
    scores = scores * head_size ** (-0.5)
    pos_bias = jnp.dot(rel_table, offset_table().T, precision=lax.Precision.HIGHEST).reshape(HEADS, WIN * WIN, WIN * WIN)
    labels = to_windows(jnp.broadcast_to(region[:, None, None], (rows_in, cols_in, 1)))[:, :, 0]
    allowed = labels[:, None, :, None] == labels[:, None, None, :]
    scores = jnp.where(allowed, scores + pos_bias[None], -1000000000.0)
    row_peak = lax.stop_gradient(lax.optimization_barrier(jnp.max(scores, axis=-1, keepdims=True)))
    exp_scores = jnp.exp(scores - row_peak)
    weights = (exp_scores / lax.optimization_barrier(jnp.sum(exp_scores, axis=-1, keepdims=True))).astype(jnp.bfloat16)
    mixed_heads = jnp.einsum('nhqk,nkhd->nqhd', weights.astype(jnp.float32), triple[:, :, 2].astype(jnp.float32))
    mixed_heads = mixed_heads.astype(jnp.bfloat16).reshape(-1, C)
    attended = jnp.dot(mixed_heads, proj_weight, preferred_element_type=jnp.float32).reshape(-1, WIN * WIN, C)
    hidden = signal + from_windows(attended, rows_in, cols_in)
    flat_rows = hidden.reshape(-1, C)
    lifted = jax.nn.gelu(jnp.dot(layer_normed(flat_rows).astype(jnp.bfloat16), up_weight, preferred_element_type=jnp.float32)).astype(jnp.bfloat16)
    mixed_out = flat_rows + jnp.dot(lifted, down_weight, preferred_element_type=jnp.float32)
    gdn_power = gdn_beta + jnp.dot(mixed_out * mixed_out, gdn_gamma, precision=lax.Precision.HIGHEST)
    return (mixed_out * lax.rsqrt(gdn_power)).reshape(rows_in, cols_in, C).astype(jnp.bfloat16)

def to_tiles(grid_data):
    grid_data = grid_data.reshape(N_LAT, H_DEV, N_LON, W_DEV, C)
    return grid_data.transpose(0, 2, 1, 3, 4).reshape(N_LAT * N_LON, H_DEV, W_DEV, C)

def from_tiles(grid_data):
    grid_data = grid_data.reshape(N_LAT, N_LON, H_DEV, W_DEV, C)
    return grid_data.transpose(0, 2, 1, 3, 4).reshape(NLAT, NLON, C)

def reference(signal, cotangent, qkv_weight, proj_weight, up_weight, down_weight, gdn_gamma, gdn_beta, rel_table):
    params = (qkv_weight, proj_weight, up_weight, down_weight, gdn_gamma, gdn_beta, rel_table)
    first_params = tuple((member[0] for member in params))
    second = tuple((member[1] for member in params))
    image_in = signal.reshape(NLAT, NLON, C)
    target = cotangent.reshape(NLAT, NLON, C)
    flat_region = jnp.zeros((H_DEV,), jnp.int32)
    row_index = jnp.arange(H_DEV, dtype=jnp.int32)
    sectioned = from_tiles(lax.map(lambda tile_in: swin_block(tile_in, first_params, flat_region), to_tiles(image_in)))
    rolled = jnp.roll(sectioned, (-SHIFT, -SHIFT), axis=(0, 1))
    rolled_target = jnp.roll(target, (-SHIFT, -SHIFT), axis=(0, 1))
    band_index = jnp.arange(N_LAT * N_LON, dtype=jnp.int32) // N_LON

    def second_step(totals, inputs):
        tile_in, target_tile, band_row = inputs
        region = ((band_row == N_LAT - 1) & (row_index >= H_DEV - SHIFT)).astype(jnp.int32)
        output, backward = jax.vjp(lambda piece_in, weights: swin_block(piece_in, weights, region), tile_in, second)
        piece_grad, weight_grads = backward(target_tile)
        totals = tuple((total + grad_part.astype(jnp.float32) for total, grad_part in zip(totals, weight_grads)))
        return (totals, (output, piece_grad))
    zero_second = tuple((jnp.zeros(member.shape, jnp.float32) for member in second))
    second_total, (outputs, piece_grads) = lax.scan(second_step, zero_second, (to_tiles(rolled), to_tiles(rolled_target), band_index))
    decoded = jnp.roll(from_tiles(outputs), (SHIFT, SHIFT), axis=(0, 1))
    back_grad = jnp.roll(from_tiles(piece_grads), (SHIFT, SHIFT), axis=(0, 1))

    def first_step(totals, inputs):
        tile_in, target_tile = inputs
        output, backward = jax.vjp(lambda piece_in, weights: swin_block(piece_in, weights, flat_region), tile_in, first_params)
        piece_grad, weight_grads = backward(target_tile)
        totals = tuple((total + grad_part.astype(jnp.float32) for total, grad_part in zip(totals, weight_grads)))
        return (totals, piece_grad)
    zero_first = tuple((jnp.zeros(member.shape, jnp.float32) for member in first_params))
    first_total, input_tiles = lax.scan(first_step, zero_first, (to_tiles(image_in), to_tiles(back_grad)))
    signal_grad = from_tiles(input_tiles)
    grad_scale = 1.0 / math.sqrt(PIXELS)
    grads = tuple((jnp.stack([one_part, two_part]) * grad_scale for one_part, two_part in zip(first_total, second_total)))
    return (decoded.reshape(NLAT, NLON * C), signal_grad.reshape(NLAT, NLON * C), grads[0], grads[1], grads[2], grads[3], grads[4], grads[5], grads[6])
```

```python
import functools
import math

import jax
import jax.numpy as jnp
from jax import lax
from jax.experimental import pallas as pl
from jax.experimental.pallas import tpu as pltpu
from jax.sharding import PartitionSpec as P

C = 96
HEADS = 3
HEAD = 32
HID = 384
WIN = 8
RELS = 225
SLOTS = 256
PIX = 512
HALF = 256
UNIT = 16
WINDOWS = 8
TOKENS = 64
ROWS = 1024
TILE = 8
EPS = 1e-05
GELU_A = math.sqrt(2.0 / math.pi)
GELU_B = 0.044715
MESH = pl.DeviceIdType.MESH
F32 = jnp.float32
BF16 = jnp.bfloat16


def iota(shape, dim):
    return lax.broadcasted_iota(jnp.int32, shape, dim)


def dot(a, b, over=(1, 0)):
    return lax.dot_general(a, b, (((over[0],), (over[1],)), ((), ())), preferred_element_type=F32)


def dot_split(a, b):
    high = a.astype(BF16)
    rest = a - high.astype(F32)
    middle = rest.astype(BF16)
    low = (rest - middle.astype(F32)).astype(BF16)
    return dot(high, b) + dot(middle, b) + dot(low, b)


def row_mean(a):
    return jnp.sum(a, axis=-1, keepdims=True) * (1.0 / C)


def normalise(v):
    center = v - row_mean(v)
    scale = lax.rsqrt(row_mean(center * center) + EPS)
    return center * scale, scale


def norm_back(grad, hat, scale):
    return scale * (grad - row_mean(grad) - hat * row_mean(grad * hat))


def stack_heads(a):
    head_of = iota(a.shape, 1) // HEAD
    zero = jnp.zeros_like(a)
    return jnp.concatenate([jnp.where(head_of == h, a, zero) for h in range(HEADS)], axis=0)


def merge_heads(a):
    parts = [a[h * TOKENS : (h + 1) * TOKENS] for h in range(HEADS)]
    head_of = iota((TOKENS, C), 1) // HEAD
    return jnp.where(head_of == 0, parts[0], jnp.where(head_of == 1, parts[1], parts[2]))


def window(ref, w):
    step = TOKENS // 2
    upper = ref[w * step : (w + 1) * step, :]
    lower = ref[HALF + w * step : HALF + (w + 1) * step, :]
    return jnp.concatenate([upper, lower], axis=0)


def put_window(ref, w, value):
    step = TOKENS // 2
    ref[w * step : (w + 1) * step, :] = value[:step].astype(ref.dtype)
    ref[HALF + w * step : HALF + (w + 1) * step, :] = value[step:].astype(ref.dtype)


def unfold(src, dst):
    low = iota((WIN, C), 0) < 4
    for group in range(16):
        part = src[:, group * 4 * C : (group + 1) * 4 * C].astype(F32)
        for pair in range(2):
            one = part[:, (2 * pair) * C : (2 * pair + 1) * C]
            two = part[:, (2 * pair + 1) * C : (2 * pair + 2) * C]
            at = (group * 2 + pair) * 8
            dst[at : at + 8, :] = jnp.where(low, one, pltpu.roll(two, 4, 0)).astype(dst.dtype)
            dst[HALF + at : HALF + at + 8, :] = jnp.where(low, pltpu.roll(one, 4, 0), two).astype(dst.dtype)


def fold(value, dst):
    low = iota((WIN, C), 0) < 4
    for group in range(16):
        parts = []
        for pair in range(2):
            at = (group * 2 + pair) * 8
            upper = value[at : at + 8]
            lower = value[HALF + at : HALF + at + 8]
            parts.append(jnp.where(low, upper, pltpu.roll(lower, 4, 0)))
            parts.append(jnp.where(low, pltpu.roll(upper, 4, 0), lower))
        dst[:, group * 4 * C : (group + 1) * 4 * C] = jnp.concatenate(parts, axis=1).astype(dst.dtype)


def rel_slots():
    entry = iota((RELS, SLOTS), 0)
    slot = iota((RELS, SLOTS), 1)
    return ((entry // 15 == slot % 16) & (entry % 15 == slot // 16)).astype(F32)


def spread_queries():
    query = iota((HEADS * TOKENS, HEADS * 128), 0)
    place = iota((HEADS * TOKENS, HEADS * 128), 1)
    inside = query % TOKENS
    row = (inside // 32) * 4 + inside % 4
    column = (inside % 32) // 4
    return ((query // TOKENS) * 128 + column * 16 + row == place).astype(F32)


def build_bias(table, bias):
    slots = dot_split(table, rel_slots().astype(BF16))
    sub = iota((8, SLOTS), 0)
    heads = []
    for h in range(HEADS):
        line = jnp.broadcast_to(slots[h : h + 1], (8, SLOTS))
        skew = line
        for s in range(1, 8):
            skew = jnp.where(sub == s, pltpu.roll(line, 16 * (s // 4) + s % 4, 1), skew)
        groups = []
        for g in range(8):
            turn = SLOTS - 119 + 32 * (g % 4) + 4 * (g // 4)
            groups.append(pltpu.roll(skew, turn % SLOTS, 1)[:, :128])
        heads.append(jnp.concatenate(groups, axis=0))
    wide = jnp.concatenate(heads, axis=1)
    back = spread_queries().astype(BF16)
    high = wide.astype(BF16)
    rest = wide - high.astype(F32)
    middle = rest.astype(BF16)
    low = (rest - middle.astype(F32)).astype(BF16)
    bias[...] = dot(high, back, (1, 1)) + dot(middle, back, (1, 1)) + dot(low, back, (1, 1))


def table_slots(total):
    wide = dot(total.astype(BF16), spread_queries().astype(BF16))
    sub = iota((8, SLOTS), 0)
    blank = jnp.zeros((8, 128), F32)
    lines = []
    for h in range(HEADS):
        skew = jnp.zeros((8, SLOTS), F32)
        for g in range(8):
            part = jnp.concatenate([wide[8 * g : 8 * g + 8, 128 * h : 128 * h + 128], blank], axis=1)
            skew = skew + pltpu.roll(part, 119 - 32 * (g % 4) - 4 * (g // 4), 1)
        line = skew
        for s in range(1, 8):
            line = jnp.where(sub == s, pltpu.roll(skew, SLOTS - 16 * (s // 4) - s % 4, 1), line)
        lines.append(jnp.sum(line, axis=0, keepdims=True))
    return lines


def forward(x, weights, saved, blocked):
    (wq, wk, wv), wproj, wup, wdown, gamma, beta = weights
    hat, scale = normalise(x)
    saved.hat1[...] = hat
    saved.scale1[...] = scale
    normed = hat.astype(BF16)
    saved.query[...] = dot(normed, wq).astype(BF16)
    saved.key[...] = dot(normed, wk).astype(BF16)
    saved.value[...] = dot(normed, wv).astype(BF16)
    bias = saved.bias[...]
    for w in range(WINDOWS):
        query = stack_heads(window(saved.query, w))
        score = dot(window(saved.key, w), query, (1, 1)) * (HEAD**-0.5) + bias
        if blocked is not None:
            score = jnp.where(blocked, -1e9, score)
        raised = jnp.exp(score - jnp.max(score, axis=0, keepdims=True))
        attn = raised / jnp.sum(raised, axis=0, keepdims=True)
        saved.attn[w] = attn
        mixed = merge_heads(dot(attn.astype(BF16), window(saved.value, w), (0, 0)))
        put_window(saved.mixed, w, mixed)
    hidden = x + dot(saved.mixed[...], wproj)
    hat, scale = normalise(hidden)
    saved.hat2[...] = hat
    saved.scale2[...] = scale
    up = dot(hat.astype(BF16), wup)
    square = up * up
    bent = jnp.tanh(GELU_A * up * (1.0 + GELU_B * square))
    half = 0.5 * (1.0 + bent)
    lifted = (up * half).astype(BF16)
    saved.lifted[...] = lifted
    saved.slope[...] = half + 0.5 * up * (1.0 - bent * bent) * (GELU_A * (1.0 + 3.0 * GELU_B * square))
    gdn = hidden + dot(lifted, wdown)
    power = beta + dot((gdn * gdn).astype(BF16), gamma)
    root = lax.rsqrt(power)
    saved.gdn[...] = gdn
    saved.root[...] = root
    return gdn * root


def backward(grad, weights, saved, pack):
    (wq, wk, wv), wproj, wup, wdown, gamma, beta = weights
    gdn = saved.gdn[...]
    root = saved.root[...]
    dpower = -0.5 * grad * gdn * (root * root * root)
    dpower_16 = dpower.astype(BF16)
    gamma_grad = dot((gdn * gdn).astype(BF16), dpower_16, (0, 0))
    for i in range(3):
        pack[C * i : C * (i + 1), C:128] = gamma_grad[:, 32 * i : 32 * (i + 1)].astype(BF16)
    beta_grad = jnp.sum(dpower, axis=0, keepdims=True)
    dgdn = grad * root + 2.0 * gdn * dot(dpower_16, gamma, (1, 1))
    dgdn_16 = dgdn.astype(BF16)
    down_grad = dot(dgdn_16, saved.lifted[...], (0, 0))
    for i in range(3):
        pack[672 + C * i : 672 + C * (i + 1), :] = down_grad[:, 128 * i : 128 * (i + 1)].astype(BF16)
    dup = (dot(dgdn_16, wdown, (1, 1)) * saved.slope[...]).astype(BF16)
    hat2 = saved.hat2[...]
    up_grad = dot(hat2.astype(BF16), dup, (0, 0))
    for i in range(3):
        pack[384 + C * i : 384 + C * (i + 1), :] = up_grad[:, 128 * i : 128 * (i + 1)].astype(BF16)
    dhidden = dgdn + norm_back(dot(dup, wup, (1, 1)), hat2, saved.scale2[...])
    dhidden_16 = dhidden.astype(BF16)
    proj_grad = dot(saved.mixed[...], dhidden_16, (0, 0))
    pack[288:384, 0:C] = proj_grad.astype(BF16)
    saved.dmixed[...] = dot(dhidden_16, wproj, (1, 1)).astype(BF16)
    total = jnp.zeros((TOKENS, HEADS * TOKENS), F32)
    for w in range(WINDOWS):
        dmixed = stack_heads(window(saved.dmixed, w))
        attn = saved.attn[w]
        dattn = dot(window(saved.value, w), dmixed, (1, 1))
        put_window(saved.dvalue, w, dot(attn.astype(BF16), dmixed))
        dscore = attn * (dattn - jnp.sum(attn * dattn, axis=0, keepdims=True))
        total = total + dscore
        dscore = (dscore * (HEAD**-0.5)).astype(BF16)
        put_window(saved.dkey, w, dot(dscore, stack_heads(window(saved.query, w))))
        put_window(saved.dquery, w, merge_heads(dot(dscore, window(saved.key, w), (0, 0))))
    lines = table_slots(total)
    hat1 = saved.hat1[...]
    normed = hat1.astype(BF16)
    dnormed = jnp.zeros((PIX, C), F32)
    for i, (part, weight) in enumerate(((saved.dquery, wq), (saved.dkey, wk), (saved.dvalue, wv))):
        piece = part[...]
        pack[C * i : C * (i + 1), 0:C] = dot(normed, piece, (0, 0)).astype(BF16)
        dnormed = dnormed + dot(piece, weight, (1, 1))
    edge = jnp.concatenate([beta_grad, jnp.zeros((1, 128 - C), F32)], axis=1)
    rows = [edge] + [line[:, 128 * i : 128 * (i + 1)] for line in lines for i in range(2)]
    rows.append(jnp.zeros((ROWS - 967, 128), F32))
    pack[960:ROWS, :] = jnp.concatenate(rows, axis=0).astype(BF16)
    return dhidden + norm_back(dnormed, hat1, saved.scale1[...])


class Saved:
    names = {
        "hat1": ((PIX, C), F32),
        "scale1": ((PIX, 1), F32),
        "query": ((PIX, C), BF16),
        "key": ((PIX, C), BF16),
        "value": ((PIX, C), BF16),
        "bias": ((TOKENS, HEADS * TOKENS), F32),
        "attn": ((WINDOWS, TOKENS, HEADS * TOKENS), F32),
        "mixed": ((PIX, C), BF16),
        "hat2": ((PIX, C), F32),
        "scale2": ((PIX, 1), F32),
        "lifted": ((PIX, HID), BF16),
        "slope": ((PIX, HID), F32),
        "gdn": ((PIX, C), F32),
        "root": ((PIX, C), F32),
        "dmixed": ((PIX, C), BF16),
        "dquery": ((PIX, C), BF16),
        "dkey": ((PIX, C), BF16),
        "dvalue": ((PIX, C), BF16),
    }

    def __init__(self, refs):
        for name, ref in zip(Saved.names, refs):
            setattr(self, name, ref)


def copy_to(src, dst, send, recv, device):
    return pltpu.make_async_remote_copy(
        src_ref=src, dst_ref=dst, send_sem=send, recv_sem=recv, device_id=device, device_id_type=MESH
    )


def read_weights(b, refs):
    wqkv, wproj, wup, wdown, gamma, beta = refs
    whole = wqkv[b].astype(F32)
    parts = tuple(whole[:, C * i : C * (i + 1)].astype(BF16) for i in range(3))
    return parts, wproj[b], wup[b], wdown[b], gamma[b].astype(BF16), beta[b : b + 1, :]


class Exchange:
    def __init__(self, b, n_lat, n_lon, pack, first, chunk, second, third, fourth, sems):
        self.b, self.n_lat, self.n_lon = b, n_lat, n_lon
        self.pack, self.first, self.chunk = pack, first, chunk
        self.second, self.third, self.fourth = second, third, fourth
        self.sems = sems
        self.rows = ROWS // n_lat
        self.tiles = self.rows // TILE
        self.owners = min(self.tiles, n_lon // 2)
        self.deep = self.rows // self.owners
        self.lat, self.lon = lax.axis_index("lat"), lax.axis_index("lon")

    def owner(self, t):
        return 2 * t + self.b

    def piece(self, ref, i):
        return ref.at[pl.ds(pl.multiple_of(i * self.rows, self.rows), self.rows), :]

    def lat_copy(self, o):
        to = lax.rem(self.lat + o, self.n_lat)
        send, recv = self.sems[0], self.sems[1]
        return copy_to(self.piece(self.pack, to), self.first.at[o], send.at[o], recv.at[o], (to, self.lon))

    def start_lat(self):
        def body(o, _):
            self.lat_copy(o).start()
            return 0

        lax.fori_loop(1, self.n_lat, body, 0)

    def add_lat(self):
        def body(o, _):
            self.lat_copy(o).wait()
            return 0

        lax.fori_loop(1, self.n_lat, body, 0)
        at = pl.ds(pl.multiple_of(self.lat * self.rows, self.rows), self.rows)
        total = self.pack[at, :].astype(F32)
        for o in range(1, self.n_lat):
            total = total + self.first[o].astype(F32)
        self.chunk[...] = total.reshape(self.owners, self.deep, 128)

    def lon_copy(self, t):
        send, recv = self.sems[2], self.sems[3]
        return copy_to(
            self.chunk.at[t], self.second.at[self.lon], send.at[t], recv.at[self.lon], (self.lat, self.owner(t))
        )

    def start_lon(self):
        def body(t, _):
            @pl.when(self.owner(t) != self.lon)
            def _():
                self.lon_copy(t).start()

            return 0

        lax.fori_loop(0, self.owners, body, 0)

    def gather_copy(self, o):
        send, recv = self.sems[4], self.sems[5]
        to = lax.rem(self.lon + o, self.n_lon)
        mine = self.lon // 2
        return copy_to(self.third.at[mine], self.third.at[mine], send.at[o], recv.at[mine], (self.lat, to))

    def add_lon(self, factor):
        def sent(t, _):
            @pl.when(self.owner(t) != self.lon)
            def _():
                self.lon_copy(t).wait_send()

            return 0

        lax.fori_loop(0, self.owners, sent, 0)

        @pl.when(lax.rem(self.lon, 2) == self.b)
        def _():
            mine = self.lon // 2

            def arrived(o, _):
                source = lax.rem(self.lon + o, self.n_lon)
                pltpu.make_async_copy(self.second.at[source], self.second.at[source], self.sems[3].at[source]).wait()
                return 0

            lax.fori_loop(1, self.n_lon, arrived, 0)
            self.second[self.lon] = self.chunk[mine]
            total = self.second[0]
            for i in range(1, self.n_lon):
                total = total + self.second[i]
            self.third[mine] = total * factor

            def give(o, _):
                self.gather_copy(o).start()
                return 0

            lax.fori_loop(1, self.n_lon, give, 0)

    def fourth_copy(self, o):
        to = lax.rem(self.lat + o, self.n_lat)
        send, recv = self.sems[6], self.sems[7]
        place = self.piece(self.fourth, self.lat)
        return copy_to(place, place, send.at[o], recv.at[self.lat], (to, self.lon))

    def finish_lon(self):
        @pl.when(lax.rem(self.lon, 2) == self.b)
        def _():
            def sent(o, _):
                self.gather_copy(o).wait_send()
                return 0

            lax.fori_loop(1, self.n_lon, sent, 0)

        def arrived(t, _):
            @pl.when(self.owner(t) != self.lon)
            def _():
                pltpu.make_async_copy(self.third.at[t], self.third.at[t], self.sems[5].at[t]).wait()

            return 0

        lax.fori_loop(0, self.owners, arrived, 0)
        at = pl.ds(pl.multiple_of(self.lat * self.rows, self.rows), self.rows)
        self.fourth[at, :] = self.third[...].reshape(self.rows, 128).astype(BF16)

        def give(o, _):
            self.fourth_copy(o).start()
            return 0

        lax.fori_loop(1, self.n_lat, give, 0)

    def finish_lat(self):
        def body(o, _):
            self.fourth_copy(o).wait_send()
            source = lax.rem(self.lat + o, self.n_lat)
            place = self.piece(self.fourth, source)
            pltpu.make_async_copy(place, place, self.sems[7].at[source]).wait()
            return 0

        lax.fori_loop(1, self.n_lat, body, 0)


def exchange_scratch(n_lat, n_lon):
    rows = ROWS // n_lat
    owners = min(rows // TILE, n_lon // 2)
    deep = rows // owners
    dma = pltpu.SemaphoreType.DMA
    return [
        pltpu.VMEM((ROWS, 128), BF16),
        pltpu.VMEM((n_lat, rows, 128), BF16),
        pltpu.VMEM((owners, deep, 128), F32),
        pltpu.VMEM((n_lon, deep, 128), F32),
        pltpu.VMEM((owners, deep, 128), F32),
        pltpu.VMEM((ROWS, 128), BF16),
        dma((n_lat,)),
        dma((n_lat,)),
        dma((owners,)),
        dma((n_lon,)),
        dma((n_lon,)),
        dma((owners,)),
        dma((n_lat,)),
        dma((n_lat,)),
    ]


def unpack(b, total, outs):
    qkv, proj, up, down, gamma, beta, table = outs
    first = total[0:288, :].astype(F32)
    parts = [first[C * i : C * (i + 1)] for i in range(3)]
    qkv[b] = jnp.concatenate([part[:, 0:C] for part in parts], axis=1)
    gamma[b] = jnp.concatenate([part[:, C:128] for part in parts], axis=1)
    proj[b] = total[288:384, 0:C].astype(F32)
    for i in range(3):
        up[b, :, 128 * i : 128 * (i + 1)] = total[384 + C * i : 384 + C * (i + 1), :].astype(F32)
        block = total[672 + C * i : 672 + C * (i + 1), :].astype(F32)
        down[b, 128 * i : 128 * (i + 1), :] = block.T
    edge = total[960:976, :].astype(F32)
    beta[b : b + 1, :] = edge[0:1, 0:C]
    lines = [jnp.concatenate([edge[1 + 2 * h : 2 + 2 * h], edge[2 + 2 * h : 3 + 2 * h]], axis=1) for h in range(HEADS)]
    table[b] = dot(jnp.concatenate(lines, axis=0).astype(BF16), rel_slots().astype(BF16), (1, 1))


def kernel(n_lat, n_lon, *refs):
    refs = list(refs)

    def take(count):
        taken = refs[:count]
        del refs[:count]
        return taken

    sig, cot = take(2)
    weight_refs = take(6)
    (table,) = take(1)
    decoded, sgrad = take(2)
    grad_outs = take(7)
    saved = [Saved(take(len(Saved.names))) for _ in range(2)]
    field, send_out, send_cot, send_dec, send_grad = take(5)
    south, east, corner, halo_send, halo_recv = take(5)
    exchanges = []
    for b in range(2):
        parts = take(14)
        exchanges.append(Exchange(b, n_lat, n_lon, *parts[:6], parts[6:]))
    lat, lon = lax.axis_index("lat"), lax.axis_index("lon")
    above, below = lax.rem(lat + n_lat - 1, n_lat), lax.rem(lat + 1, n_lat)
    west, easterly = lax.rem(lon + n_lon - 1, n_lon), lax.rem(lon + 1, n_lon)

    barrier = pltpu.get_barrier_semaphore()

    def greet(device):
        pl.semaphore_signal(barrier, inc=1, device_id=device, device_id_type=MESH)

    def greet_lat(o, _):
        greet((lax.rem(lat + o, n_lat), lon))
        return 0

    def greet_lon(o, _):
        greet((lat, lax.rem(lon + o, n_lon)))
        return 0

    lax.fori_loop(1, n_lat, greet_lat, 0)
    lax.fori_loop(1, n_lon, greet_lon, 0)
    greet((above, west))
    greet((below, easterly))

    def halo(i, whole, whole_rows, side, side_rows, both_rows, devices):
        copies = []
        rows = (whole_rows, side_rows, both_rows)
        targets = (south, east, corner)
        for j in range(3):
            src = whole.at[pl.ds(rows[j][0], rows[j][1]), :]
            k = 3 * i + j
            copies.append(copy_to(src, targets[j].at[i], halo_send.at[k], halo_recv.at[k], devices[j]))
        return copies

    def up_halo(i, ref):
        return halo(
            i, ref, (0, HALF), ref, (HALF, UNIT), (0, UNIT), ((above, lon), (lat, west), (above, west))
        )

    def down_halo(i, ref):
        return halo(
            i,
            ref,
            (HALF, HALF),
            ref,
            (HALF - UNIT, UNIT),
            (PIX - UNIT, UNIT),
            ((below, lon), (lat, easterly), (below, easterly)),
        )

    def shifted(i, ref):
        parts = [ref[HALF + UNIT : PIX, :], east[i], south[i, UNIT:HALF, :], corner[i]]
        return jnp.concatenate([part.astype(F32) for part in parts], axis=0)

    def unshifted(i, ref):
        parts = [corner[i], south[i, 0 : HALF - UNIT, :], east[i], ref[0 : HALF - UNIT, :]]
        return jnp.concatenate([part.astype(F32) for part in parts], axis=0)

    unfold(sig, field)
    unfold(cot, send_cot)
    for b in range(2):
        build_bias(table[b], saved[b].bias)
    weights = [read_weights(b, weight_refs) for b in range(2)]
    output = forward(field[...], weights[0], saved[0], None)
    send_out[...] = output.astype(BF16)

    pl.semaphore_wait(barrier, n_lat + n_lon)
    out_copies = up_halo(0, send_out)
    cot_copies = up_halo(1, send_cot)
    for copy in out_copies + cot_copies:
        copy.start()
    for copy in out_copies:
        copy.wait()
    is_last = (lat == n_lat - 1).astype(jnp.int32)
    shape = (TOKENS, HEADS * TOKENS)
    differ = (iota(shape, 0) // 32 != (iota(shape, 1) % TOKENS) // 32).astype(jnp.int32)
    blocked = differ * is_last > 0
    output = forward(shifted(0, send_out), weights[1], saved[1], blocked)
    send_dec[...] = output.astype(BF16)
    dec_copies = down_halo(2, send_dec)
    for copy in dec_copies:
        copy.start()
    for copy in cot_copies:
        copy.wait()
    back = backward(shifted(1, send_cot), weights[1], saved[1], exchanges[1].pack)
    send_grad[...] = back.astype(BF16)
    grad_copies = down_halo(3, send_grad)
    for copy in grad_copies:
        copy.start()
    exchanges[1].start_lat()
    for copy in dec_copies:
        copy.wait()
    fold(unshifted(2, send_dec), decoded)
    for copy in grad_copies:
        copy.wait()
    back = backward(unshifted(3, send_grad), weights[0], saved[0], exchanges[0].pack)
    fold(back, sgrad)
    exchanges[0].start_lat()
    factor = 1.0 / math.sqrt(PIX * n_lat * n_lon)
    for step in ("add_lat", "start_lon", "add_lon", "finish_lon", "finish_lat"):
        for b in (1, 0):
            method = getattr(exchanges[b], step)
            if step == "add_lon":
                method(factor)
            else:
                method()
    for b in (1, 0):
        unpack(b, exchanges[b].fourth, grad_outs)


def solution(mesh):
    n_lat, n_lon = mesh.shape["lat"], mesh.shape["lon"]

    def per_device(sig, cot, wqkv, wproj, wup, wdown, gamma, beta, table):
        dma = pltpu.SemaphoreType.DMA
        saved = [pltpu.VMEM(shape, kind) for shape, kind in Saved.names.values()]
        scratch = saved + saved
        scratch += [pltpu.VMEM((PIX, C), F32)] + [pltpu.VMEM((PIX, C), BF16)] * 4
        scratch += [
            pltpu.VMEM((4, HALF, C), BF16),
            pltpu.VMEM((4, UNIT, C), BF16),
            pltpu.VMEM((4, UNIT, C), BF16),
            dma((12,)),
            dma((12,)),
        ]
        for _ in range(2):
            scratch += exchange_scratch(n_lat, n_lon)
        shapes = [(sig.shape, BF16), (cot.shape, BF16)]
        shapes += [(leaf.shape, F32) for leaf in (wqkv, wproj, wup, wdown, gamma, beta, table)]
        vmem = pl.BlockSpec(memory_space=pltpu.VMEM)
        return pl.pallas_call(
            functools.partial(kernel, n_lat, n_lon),
            out_shape=[jax.ShapeDtypeStruct(shape, kind) for shape, kind in shapes],
            in_specs=[vmem] * 9,
            out_specs=[vmem] * 9,
            scratch_shapes=scratch,
            compiler_params=pltpu.CompilerParams(
                collective_id=0, has_side_effects=True, vmem_limit_bytes=48 * 1024 * 1024
            ),
        )(sig, cot, wqkv, wproj, wup, wdown, gamma, beta, table)

    in_specs = (P("lat", "lon"), P("lat", "lon"), P(), P(), P(), P(), P(), P(), P())
    out_specs = (P("lat", "lon"), P("lat", "lon"), P(), P(), P(), P(), P(), P(), P())
    return jax.shard_map(per_device, mesh=mesh, in_specs=in_specs, out_specs=out_specs, check_vma=False)
```

```python
import functools
import math

import jax
import jax.numpy as jnp
from jax import lax
from jax.experimental import pallas as pl
from jax.experimental.pallas import tpu as pltpu
from jax.sharding import PartitionSpec as P

C = 96
HEADS = 3
HEAD = 32
HID = 384
WIN = 8
RELS = 225
SLOTS = 256
PIX = 512
HALF = 256
UNIT = 16
WINDOWS = 8
TOKENS = 64
ROWS = 1024
QUAD = 4
EPS = 1e-05
GELU_A = math.sqrt(2.0 / math.pi)
GELU_B = 0.044715
MESH = pl.DeviceIdType.MESH
F32 = jnp.float32
BF16 = jnp.bfloat16


def iota(shape, dim):
    return lax.broadcasted_iota(jnp.int32, shape, dim)


def dot(a, b, over=(1, 0)):
    return lax.dot_general(a, b, (((over[0],), (over[1],)), ((), ())), preferred_element_type=F32)


def dot_split(a, b):
    high = a.astype(BF16)
    rest = a - high.astype(F32)
    middle = rest.astype(BF16)
    low = (rest - middle.astype(F32)).astype(BF16)
    return dot(high, b) + dot(middle, b) + dot(low, b)


def row_mean(a):
    return jnp.sum(a, axis=-1, keepdims=True) * (1.0 / C)


def normalise(v):
    center = v - row_mean(v)
    scale = lax.rsqrt(row_mean(center * center) + EPS)
    return center * scale, scale


def norm_back(grad, hat, scale):
    return scale * (grad - row_mean(grad) - hat * row_mean(grad * hat))


def stack_heads(a):
    head_of = iota(a.shape, 1) // HEAD
    zero = jnp.zeros_like(a)
    return jnp.concatenate([jnp.where(head_of == h, a, zero) for h in range(HEADS)], axis=0)


def merge_heads(a):
    parts = [a[h * TOKENS : (h + 1) * TOKENS] for h in range(HEADS)]
    head_of = iota((TOKENS, C), 1) // HEAD
    return jnp.where(head_of == 0, parts[0], jnp.where(head_of == 1, parts[1], parts[2]))


def window(ref, w):
    step = TOKENS // 2
    upper = ref[w * step : (w + 1) * step, :]
    lower = ref[HALF + w * step : HALF + (w + 1) * step, :]
    return jnp.concatenate([upper, lower], axis=0)


def put_window(ref, w, value):
    step = TOKENS // 2
    ref[w * step : (w + 1) * step, :] = value[:step].astype(ref.dtype)
    ref[HALF + w * step : HALF + (w + 1) * step, :] = value[step:].astype(ref.dtype)


def unfold(src, dst):
    low = iota((WIN, C), 0) < 4
    for group in range(16):
        part = src[:, group * 4 * C : (group + 1) * 4 * C].astype(F32)
        for pair in range(2):
            one = part[:, (2 * pair) * C : (2 * pair + 1) * C]
            two = part[:, (2 * pair + 1) * C : (2 * pair + 2) * C]
            at = (group * 2 + pair) * 8
            dst[at : at + 8, :] = jnp.where(low, one, pltpu.roll(two, 4, 0)).astype(dst.dtype)
            dst[HALF + at : HALF + at + 8, :] = jnp.where(low, pltpu.roll(one, 4, 0), two).astype(dst.dtype)


def fold(value, dst):
    low = iota((WIN, C), 0) < 4
    for group in range(16):
        parts = []
        for pair in range(2):
            at = (group * 2 + pair) * 8
            upper = value[at : at + 8]
            lower = value[HALF + at : HALF + at + 8]
            parts.append(jnp.where(low, upper, pltpu.roll(lower, 4, 0)))
            parts.append(jnp.where(low, pltpu.roll(upper, 4, 0), lower))
        dst[:, group * 4 * C : (group + 1) * 4 * C] = jnp.concatenate(parts, axis=1).astype(dst.dtype)


def rel_slots():
    entry = iota((RELS, SLOTS), 0)
    slot = iota((RELS, SLOTS), 1)
    return ((entry // 15 == slot % 16) & (entry % 15 == slot // 16)).astype(F32)


def spread_queries():
    query = iota((HEADS * TOKENS, HEADS * 128), 0)
    place = iota((HEADS * TOKENS, HEADS * 128), 1)
    inside = query % TOKENS
    row = (inside // 32) * 4 + inside % 4
    column = (inside % 32) // 4
    return ((query // TOKENS) * 128 + column * 16 + row == place).astype(F32)


def build_bias(table, bias):
    slots = dot_split(table, rel_slots().astype(BF16))
    sub = iota((8, SLOTS), 0)
    heads = []
    for h in range(HEADS):
        line = jnp.broadcast_to(slots[h : h + 1], (8, SLOTS))
        skew = line
        for s in range(1, 8):
            skew = jnp.where(sub == s, pltpu.roll(line, 16 * (s // 4) + s % 4, 1), skew)
        groups = []
        for g in range(8):
            turn = SLOTS - 119 + 32 * (g % 4) + 4 * (g // 4)
            groups.append(pltpu.roll(skew, turn % SLOTS, 1)[:, :128])
        heads.append(jnp.concatenate(groups, axis=0))
    wide = jnp.concatenate(heads, axis=1)
    back = spread_queries().astype(BF16)
    high = wide.astype(BF16)
    rest = wide - high.astype(F32)
    middle = rest.astype(BF16)
    low = (rest - middle.astype(F32)).astype(BF16)
    bias[...] = dot(high, back, (1, 1)) + dot(middle, back, (1, 1)) + dot(low, back, (1, 1))


def table_slots(total):
    wide = dot(total.astype(BF16), spread_queries().astype(BF16))
    sub = iota((8, SLOTS), 0)
    blank = jnp.zeros((8, 128), F32)
    lines = []
    for h in range(HEADS):
        skew = jnp.zeros((8, SLOTS), F32)
        for g in range(8):
            part = jnp.concatenate([wide[8 * g : 8 * g + 8, 128 * h : 128 * h + 128], blank], axis=1)
            skew = skew + pltpu.roll(part, 119 - 32 * (g % 4) - 4 * (g // 4), 1)
        line = skew
        for s in range(1, 8):
            line = jnp.where(sub == s, pltpu.roll(skew, SLOTS - 16 * (s // 4) - s % 4, 1), line)
        lines.append(jnp.sum(line, axis=0, keepdims=True))
    return lines


def forward(x, weights, saved, blocked):
    (wq, wk, wv), wproj, wup, wdown, gamma, beta = weights
    hat, scale = normalise(x)
    saved.hat1[...] = hat
    saved.scale1[...] = scale
    normed = hat.astype(BF16)
    saved.query[...] = dot(normed, wq).astype(BF16)
    saved.key[...] = dot(normed, wk).astype(BF16)
    saved.value[...] = dot(normed, wv).astype(BF16)
    bias = saved.bias[...]
    for w in range(WINDOWS):
        query = stack_heads(window(saved.query, w))
        score = dot(window(saved.key, w), query, (1, 1)) * (HEAD**-0.5) + bias
        if blocked is not None:
            score = jnp.where(blocked, -1e9, score)
        raised = jnp.exp(score - jnp.max(score, axis=0, keepdims=True))
        attn = raised / jnp.sum(raised, axis=0, keepdims=True)
        saved.attn[w] = attn
        mixed = merge_heads(dot(attn.astype(BF16), window(saved.value, w), (0, 0)))
        put_window(saved.mixed, w, mixed)
    hidden = x + dot(saved.mixed[...], wproj)
    hat, scale = normalise(hidden)
    saved.hat2[...] = hat
    saved.scale2[...] = scale
    up = dot(hat.astype(BF16), wup)
    square = up * up
    bent = jnp.tanh(GELU_A * up * (1.0 + GELU_B * square))
    half = 0.5 * (1.0 + bent)
    lifted = (up * half).astype(BF16)
    saved.lifted[...] = lifted
    saved.slope[...] = half + 0.5 * up * (1.0 - bent * bent) * (GELU_A * (1.0 + 3.0 * GELU_B * square))
    gdn = hidden + dot(lifted, wdown, (1, 1))
    power = beta + dot((gdn * gdn).astype(BF16), gamma)
    root = lax.rsqrt(power)
    saved.gdn[...] = gdn
    saved.root[...] = root
    return gdn * root


def backward(grad, weights, saved, pack, early=None):
    (wq, wk, wv), wproj, wup, wdown, gamma, beta = weights
    gdn = saved.gdn[...]
    root = saved.root[...]
    dpower = -0.5 * grad * gdn * (root * root * root)
    dpower_16 = dpower.astype(BF16)
    gamma_grad = dot((gdn * gdn).astype(BF16), dpower_16, (0, 0))
    for i in range(3):
        pack[576 + C * i : 576 + C * (i + 1), C:128] = gamma_grad[:, 32 * i : 32 * (i + 1)].astype(BF16)
    beta_grad = jnp.sum(dpower, axis=0, keepdims=True)
    dgdn = grad * root + 2.0 * gdn * dot(dpower_16, gamma, (1, 1))
    dgdn_16 = dgdn.astype(BF16)
    down_grad = dot(dgdn_16, saved.lifted[...], (0, 0))
    for i in range(3):
        pack[288 + C * i : 288 + C * (i + 1), :] = down_grad[:, 128 * i : 128 * (i + 1)].astype(BF16)
    dup = (dot(dgdn_16, wdown) * saved.slope[...]).astype(BF16)
    hat2 = saved.hat2[...]
    up_grad = dot(hat2.astype(BF16), dup, (0, 0))
    for i in range(3):
        pack[C * i : C * (i + 1), :] = up_grad[:, 128 * i : 128 * (i + 1)].astype(BF16)
    dhidden = dgdn + norm_back(dot(dup, wup, (1, 1)), hat2, saved.scale2[...])
    dhidden_16 = dhidden.astype(BF16)
    proj_grad = dot(saved.mixed[...], dhidden_16, (0, 0))
    pack[864:960, 0:C] = proj_grad.astype(BF16)
    saved.dmixed[...] = dot(dhidden_16, wproj, (1, 1)).astype(BF16)
    if early is not None:
        early()
    total = jnp.zeros((TOKENS, HEADS * TOKENS), F32)
    for w in range(WINDOWS):
        dmixed = stack_heads(window(saved.dmixed, w))
        attn = saved.attn[w]
        dattn = dot(window(saved.value, w), dmixed, (1, 1))
        put_window(saved.dvalue, w, dot(attn.astype(BF16), dmixed))
        dscore = attn * (dattn - jnp.sum(attn * dattn, axis=0, keepdims=True))
        total = total + dscore
        dscore = (dscore * (HEAD**-0.5)).astype(BF16)
        put_window(saved.dkey, w, dot(dscore, stack_heads(window(saved.query, w))))
        put_window(saved.dquery, w, merge_heads(dot(dscore, window(saved.key, w), (0, 0))))
    lines = table_slots(total)
    hat1 = saved.hat1[...]
    normed = hat1.astype(BF16)
    dnormed = jnp.zeros((PIX, C), F32)
    for i, (part, weight) in enumerate(((saved.dquery, wq), (saved.dkey, wk), (saved.dvalue, wv))):
        piece = part[...]
        pack[576 + C * i : 576 + C * (i + 1), 0:C] = dot(normed, piece, (0, 0)).astype(BF16)
        dnormed = dnormed + dot(piece, weight, (1, 1))
    edge = jnp.concatenate([beta_grad, jnp.zeros((1, 128 - C), F32)], axis=1)
    rows = [edge] + [line[:, 128 * i : 128 * (i + 1)] for line in lines for i in range(2)]
    rows.append(jnp.zeros((ROWS - 967, 128), F32))
    pack[960:ROWS, :] = jnp.concatenate(rows, axis=0).astype(BF16)
    return dhidden + norm_back(dnormed, hat1, saved.scale1[...])


class Saved:
    names = {
        "hat1": ((PIX, C), F32),
        "scale1": ((PIX, 1), F32),
        "query": ((PIX, C), BF16),
        "key": ((PIX, C), BF16),
        "value": ((PIX, C), BF16),
        "bias": ((TOKENS, HEADS * TOKENS), F32),
        "attn": ((WINDOWS, TOKENS, HEADS * TOKENS), F32),
        "mixed": ((PIX, C), BF16),
        "hat2": ((PIX, C), F32),
        "scale2": ((PIX, 1), F32),
        "lifted": ((PIX, HID), BF16),
        "slope": ((PIX, HID), F32),
        "gdn": ((PIX, C), F32),
        "root": ((PIX, C), F32),
        "dmixed": ((PIX, C), BF16),
        "dquery": ((PIX, C), BF16),
        "dkey": ((PIX, C), BF16),
        "dvalue": ((PIX, C), BF16),
    }

    def __init__(self, refs):
        for name, ref in zip(Saved.names, refs):
            setattr(self, name, ref)


def copy_to(src, dst, send, recv, device):
    return pltpu.make_async_remote_copy(
        src_ref=src, dst_ref=dst, send_sem=send, recv_sem=recv, device_id=device, device_id_type=MESH
    )


def read_weights(b, refs):
    wqkv, wproj, wup, wdown, gamma, beta = refs
    whole = wqkv[b].astype(F32)
    parts = tuple(whole[:, C * i : C * (i + 1)].astype(BF16) for i in range(3))
    return parts, wproj[b], wup[b], wdown[b], gamma[b].astype(BF16), beta[b : b + 1, :]


class Exchange:
    def __init__(self, n_lat, n_lon, base, pack, total, first, planes, sems):
        self.n_lat, self.planes_n, self.size = n_lat, n_lon // QUAD, n_lat * QUAD
        self.base, self.pack, self.total = base, pack, total
        self.first, self.planes, self.sems = first, planes, sems
        self.rows = first.shape[1]
        self.lat, lon = lax.axis_index("lat"), lax.axis_index("lon")
        self.quad, self.z = lax.rem(lon, QUAD), lon // QUAD
        self.place = self.lat * QUAD + self.quad

    def piece(self, ref, i):
        return ref.at[pl.ds(pl.multiple_of(self.base + i * self.rows, UNIT), self.rows), :]

    def in_plane(self, make):
        def body(i, _):
            step = lax.rem(4 * i + 1, 7) + 1 if self.n_lat == 8 else i + 1
            for turn in (2, 1, 3, 0):
                make(step, turn).start()
            return 0

        lax.fori_loop(0, self.n_lat - 1, body, 0)
        for turn in (2, 1, 3):
            make(0, turn).start()

    def target(self, step, turn):
        lat = lax.rem(self.lat + step, self.n_lat)
        quad = lax.rem(self.quad + turn, QUAD)
        return lat * QUAD + quad, (lat, self.z * QUAD + quad)

    def scatter_copy(self, step, turn):
        place, device = self.target(step, turn)
        slot = self.first.at[step * QUAD + turn]
        return copy_to(self.piece(self.pack, place), slot, self.sems.at[0], self.sems.at[1], device)

    def gather_copy(self, step, turn):
        _, device = self.target(step, turn)
        mine = self.piece(self.total, self.place)
        return copy_to(mine, mine, self.sems.at[4], self.sems.at[5], device)

    def plane_copy(self, step):
        z = lax.rem(self.z + step, self.planes_n)
        slot = self.planes.at[self.z]
        device = (self.lat, z * QUAD + self.quad)
        return copy_to(slot, slot, self.sems.at[2], self.sems.at[3], device)

    def wait_both(self, ref, sem):
        for i in range(2):
            pltpu.make_async_copy(ref, ref, self.sems.at[sem + i]).wait()

    def start(self):
        self.in_plane(self.scatter_copy)

    def add_plane(self):
        self.wait_both(self.first.at[pl.ds(1, self.size - 1)], 0)
        total = self.piece(self.pack, self.place)[...].astype(F32)
        for i in range(1, self.size):
            total = total + self.first[i].astype(F32)
        self.planes[self.z] = total.astype(BF16)

        def body(step, _):
            self.plane_copy(step).start()
            return 0

        lax.fori_loop(1, self.planes_n, body, 0)

    def add_all(self, factor):
        if self.planes_n > 1:
            self.wait_both(self.planes.at[pl.ds(0, self.planes_n - 1)], 2)
        total = self.planes[0].astype(F32)
        for i in range(1, self.planes_n):
            total = total + self.planes[i].astype(F32)
        self.piece(self.total, self.place)[...] = (total * factor).astype(BF16)
        self.in_plane(self.gather_copy)

    def finish(self):
        self.wait_both(self.total.at[pl.ds(self.base, (self.size - 1) * self.rows), :], 4)


def exchange_scratch(n_lat, n_lon, rows):
    rows = rows // (n_lat * QUAD)
    return [
        pltpu.VMEM((n_lat * QUAD, rows, 128), BF16),
        pltpu.VMEM((n_lon // QUAD, rows, 128), BF16),
        pltpu.SemaphoreType.DMA((6,)),
    ]


def unpack(b, total, outs):
    qkv, proj, up, down, gamma, beta, table = outs
    first = total[576:864, :].astype(F32)
    parts = [first[C * i : C * (i + 1)] for i in range(3)]
    qkv[b] = jnp.concatenate([part[:, 0:C] for part in parts], axis=1)
    gamma[b] = jnp.concatenate([part[:, C:128] for part in parts], axis=1)
    proj[b] = total[864:960, 0:C].astype(F32)
    for i in range(3):
        up[b, :, 128 * i : 128 * (i + 1)] = total[C * i : C * (i + 1), :].astype(F32)
        down[b, :, 128 * i : 128 * (i + 1)] = total[288 + C * i : 288 + C * (i + 1), :].astype(F32)
    edge = total[960:976, :].astype(F32)
    beta[b : b + 1, :] = edge[0:1, 0:C]
    lines = [jnp.concatenate([edge[1 + 2 * h : 2 + 2 * h], edge[2 + 2 * h : 3 + 2 * h]], axis=1) for h in range(HEADS)]
    slots = jnp.concatenate(lines, axis=0).astype(BF16)
    table[:, b, :] = dot(slots, rel_slots().astype(BF16), (1, 1))


def unpack_kernel(dec, sgrad, total0, total1, *refs):
    outs, staged, totals, sems = refs[:9], refs[9:16], refs[16:18], refs[18]
    loads = [pltpu.make_async_copy(src, dst, sems.at[9 + i]) for i, (src, dst) in enumerate(zip((total0, total1), totals))]
    copies = [pltpu.make_async_copy(src, dst, sems.at[i]) for i, (src, dst) in enumerate(zip((dec, sgrad) + staged, outs))]
    for copy in loads + copies[:2]:
        copy.start()
    for b in range(2):
        loads[b].wait()
        unpack(b, totals[b], staged)
    for copy in copies[2:]:
        copy.start()
    for copy in copies:
        copy.wait()


def kernel(n_lat, n_lon, *refs):
    refs = list(refs)

    def take(count):
        taken = refs[:count]
        del refs[:count]
        return taken

    hbm_args = take(9)
    results = take(4)
    args = take(9)
    (arg_sems,) = take(1)
    saved = [Saved(take(len(Saved.names))) for _ in range(2)]
    field, send_out, send_cot, send_dec, send_grad = take(5)
    south, east, corner, halo_send, halo_recv = take(5)
    packs, fields, totals = take(2), take(2), take(2)
    (result_sems,) = take(1)
    whole = Exchange(n_lat, n_lon, 0, packs[1], totals[1], *take(3))
    upper = Exchange(n_lat, n_lon, 0, packs[0], totals[0], *take(3))
    lower = Exchange(n_lat, n_lon, ROWS // 2, packs[0], totals[0], *take(3))
    lat, lon = lax.axis_index("lat"), lax.axis_index("lon")
    above, below = lax.rem(lat + n_lat - 1, n_lat), lax.rem(lat + 1, n_lat)
    west, easterly = lax.rem(lon + n_lon - 1, n_lon), lax.rem(lon + 1, n_lon)

    stores = [
        pltpu.make_async_copy(src, dst, result_sems.at[i]) for i, (src, dst) in enumerate(zip(fields + totals, results))
    ]
    loads = [pltpu.make_async_copy(src, dst, arg_sems.at[i]) for i, (src, dst) in enumerate(zip(hbm_args, args))]
    for load in loads:
        load.start()
    barrier = pltpu.get_barrier_semaphore()

    def greet(device):
        pl.semaphore_signal(barrier, inc=1, device_id=device, device_id_type=MESH)

    def greet_plane(i, _):
        _, device = whole.target(i // QUAD, lax.rem(i, QUAD))
        greet(device)
        return 0

    def greet_planes(i, _):
        greet((lat, lax.rem(lon + QUAD * i, n_lon)))
        return 0

    planes_n = n_lon // QUAD
    lax.fori_loop(1, n_lat * QUAD, greet_plane, 0)
    lax.fori_loop(1, planes_n, greet_planes, 0)
    for device in ((lat, west), (lat, easterly), (above, west), (below, easterly)):
        greet(device)
    greetings = n_lat * QUAD + planes_n + 2

    def halo(i, ref, rows, devices):
        copies = []
        for j, target in enumerate((south, east, corner)):
            src = ref.at[pl.ds(rows[j][0], rows[j][1]), :]
            k = 3 * i + j
            copies.append(copy_to(src, target.at[i], halo_send.at[k], halo_recv.at[k], devices[j]))
        return copies

    def up_halo(i, ref):
        rows = ((0, HALF), (HALF, UNIT), (0, UNIT))
        return halo(i, ref, rows, ((above, lon), (lat, west), (above, west)))

    def down_halo(i, ref):
        rows = ((HALF, HALF), (HALF - UNIT, UNIT), (PIX - UNIT, UNIT))
        return halo(i, ref, rows, ((below, lon), (lat, easterly), (below, easterly)))

    def shifted(i, ref):
        parts = [ref[HALF + UNIT : PIX, :], east[i], south[i, UNIT:HALF, :], corner[i]]
        return jnp.concatenate([part.astype(F32) for part in parts], axis=0)

    def unshifted(i, ref):
        parts = [corner[i], south[i, 0 : HALF - UNIT, :], east[i], ref[0 : HALF - UNIT, :]]
        return jnp.concatenate([part.astype(F32) for part in parts], axis=0)

    for load in loads:
        load.wait()
    sig, cot, table = args[0], args[1], args[8]
    unfold(sig, field)
    unfold(cot, send_cot)
    for b in range(2):
        build_bias(table[:, b, :], saved[b].bias)
    weights = [read_weights(b, args[2:8]) for b in range(2)]
    output = forward(field[...], weights[0], saved[0], None)
    send_out[...] = output.astype(BF16)

    pl.semaphore_wait(barrier, greetings)
    out_copies = up_halo(0, send_out)
    cot_copies = up_halo(1, send_cot)
    for copy in out_copies + cot_copies:
        copy.start()
    for copy in out_copies:
        copy.wait()
    is_last = (lat == n_lat - 1).astype(jnp.int32)
    shape = (TOKENS, HEADS * TOKENS)
    differ = (iota(shape, 0) // 32 != (iota(shape, 1) % TOKENS) // 32).astype(jnp.int32)
    blocked = differ * is_last > 0
    output = forward(shifted(0, send_out), weights[1], saved[1], blocked)
    send_dec[...] = output.astype(BF16)
    dec_copies = down_halo(2, send_dec)
    for copy in dec_copies:
        copy.start()
    for copy in cot_copies:
        copy.wait()
    back = backward(shifted(1, send_cot), weights[1], saved[1], packs[1])
    send_grad[...] = back.astype(BF16)
    grad_copies = down_halo(3, send_grad)
    for copy in grad_copies:
        copy.start()
    whole.start()
    for copy in dec_copies:
        copy.wait()
    fold(unshifted(2, send_dec), fields[0])
    stores[0].start()
    for copy in grad_copies:
        copy.wait()
    factor = 1.0 / math.sqrt(PIX * n_lat * n_lon)

    def early():
        upper.start()
        whole.add_plane()

    back = backward(unshifted(3, send_grad), weights[0], saved[0], packs[0], early)
    lower.start()
    fold(back, fields[1])
    stores[1].start()
    whole.add_all(factor)
    upper.add_plane()
    lower.add_plane()
    upper.add_all(factor)
    lower.add_all(factor)
    whole.finish()
    stores[3].start()
    upper.finish()
    lower.finish()
    stores[2].start()
    for store in stores:
        store.wait()


def solution(mesh):
    n_lat, n_lon = mesh.shape["lat"], mesh.shape["lon"]

    def per_device(sig, cot, wqkv, wproj, wup, wdown, gamma, beta, table):
        dma = pltpu.SemaphoreType.DMA
        args = (sig, cot, wqkv, wproj, wup, jnp.swapaxes(wdown, 1, 2), gamma, beta, jnp.swapaxes(table, 0, 1))
        saved = [pltpu.VMEM(shape, kind) for shape, kind in Saved.names.values()]
        scratch = [pltpu.VMEM(arg.shape, arg.dtype) for arg in args] + [dma((9,))]
        scratch += saved + saved
        scratch += [pltpu.VMEM((PIX, C), F32)] + [pltpu.VMEM((PIX, C), BF16)] * 4
        scratch += [
            pltpu.VMEM((4, HALF, C), BF16),
            pltpu.VMEM((4, UNIT, C), BF16),
            pltpu.VMEM((4, UNIT, C), BF16),
            dma((12,)),
            dma((12,)),
        ]
        scratch += [pltpu.VMEM((ROWS, 128), BF16)] * 2 + [pltpu.VMEM(sig.shape, BF16)] * 2
        scratch += [pltpu.VMEM((ROWS, 128), BF16)] * 2 + [dma((4,))]
        scratch += exchange_scratch(n_lat, n_lon, ROWS)
        scratch += exchange_scratch(n_lat, n_lon, ROWS // 2) * 2
        hbm = pl.BlockSpec(memory_space=pltpu.HBM)
        field = jax.ShapeDtypeStruct(sig.shape, BF16)
        total = jax.ShapeDtypeStruct((ROWS, 128), BF16)
        results = pl.pallas_call(
            functools.partial(kernel, n_lat, n_lon),
            out_shape=[field, field, total, total],
            in_specs=[hbm] * 9,
            out_specs=[hbm] * 4,
            scratch_shapes=scratch,
            compiler_params=pltpu.CompilerParams(
                collective_id=0, has_side_effects=True, vmem_limit_bytes=62 * 1024 * 1024
            ),
        )(*args)
        grads = [jax.ShapeDtypeStruct(leaf.shape, F32) for leaf in args[2:]]
        outs = pl.pallas_call(
            unpack_kernel,
            out_shape=[field, field] + grads,
            in_specs=[hbm] * 4,
            out_specs=[hbm] * 9,
            scratch_shapes=[pltpu.VMEM(leaf.shape, F32) for leaf in args[2:]]
            + [pltpu.VMEM((ROWS, 128), BF16)] * 2
            + [dma((11,))],
            compiler_params=pltpu.CompilerParams(vmem_limit_bytes=62 * 1024 * 1024),
        )(*results)
        decoded, sgrad, qkv, proj, up, down, gammas, betas, tables = outs
        return decoded, sgrad, qkv, proj, up, jnp.swapaxes(down, 1, 2), gammas, betas, jnp.swapaxes(tables, 0, 1)

    in_specs = (P("lat", "lon"), P("lat", "lon"), P(), P(), P(), P(), P(), P(), P())
    out_specs = (P("lat", "lon"), P("lat", "lon"), P(), P(), P(), P(), P(), P(), P())
    return jax.shard_map(per_device, mesh=mesh, in_specs=in_specs, out_specs=out_specs, check_vma=False)
```

```python
import functools
import math

import jax
import jax.numpy as jnp
from jax import lax
from jax.experimental import pallas as pl
from jax.experimental.pallas import tpu as pltpu
from jax.sharding import PartitionSpec as P

C = 96
HEADS = 3
HEAD = 32
HID = 384
WIN = 8
RELS = 225
SLOTS = 256
PIX = 512
HALF = 256
UNIT = 16
WINDOWS = 8
TOKENS = 64
ROWS = 1024
QUAD = 4
EPS = 1e-05
GELU_A = math.sqrt(2.0 / math.pi)
GELU_B = 0.044715
MESH = pl.DeviceIdType.MESH
F32 = jnp.float32
BF16 = jnp.bfloat16


def iota(shape, dim):
    return lax.broadcasted_iota(jnp.int32, shape, dim)


def dot(a, b, over=(1, 0)):
    return lax.dot_general(a, b, (((over[0],), (over[1],)), ((), ())), preferred_element_type=F32)


def dot_split(a, b):
    high = a.astype(BF16)
    rest = a - high.astype(F32)
    middle = rest.astype(BF16)
    low = (rest - middle.astype(F32)).astype(BF16)
    return dot(high, b) + dot(middle, b) + dot(low, b)


def row_mean(a):
    return jnp.sum(a, axis=-1, keepdims=True) * (1.0 / C)


def normalise(v):
    center = v - row_mean(v)
    scale = lax.rsqrt(row_mean(center * center) + EPS)
    return center * scale, scale


def norm_back(grad, hat, scale):
    return scale * (grad - row_mean(grad) - hat * row_mean(grad * hat))


def stack_heads(a):
    head_of = iota(a.shape, 1) // HEAD
    zero = jnp.zeros_like(a)
    return jnp.concatenate([jnp.where(head_of == h, a, zero) for h in range(HEADS)], axis=0)


def merge_heads(a):
    parts = [a[h * TOKENS : (h + 1) * TOKENS] for h in range(HEADS)]
    head_of = iota((TOKENS, C), 1) // HEAD
    return jnp.where(head_of == 0, parts[0], jnp.where(head_of == 1, parts[1], parts[2]))


def window(ref, w):
    step = TOKENS // 2
    upper = ref[w * step : (w + 1) * step, :]
    lower = ref[HALF + w * step : HALF + (w + 1) * step, :]
    return jnp.concatenate([upper, lower], axis=0)


def put_window(ref, w, value):
    step = TOKENS // 2
    ref[w * step : (w + 1) * step, :] = value[:step].astype(ref.dtype)
    ref[HALF + w * step : HALF + (w + 1) * step, :] = value[step:].astype(ref.dtype)


def unfold(src, dst):
    low = iota((WIN, C), 0) < 4
    for group in range(16):
        part = src[:, group * 4 * C : (group + 1) * 4 * C].astype(F32)
        for pair in range(2):
            one = part[:, (2 * pair) * C : (2 * pair + 1) * C]
            two = part[:, (2 * pair + 1) * C : (2 * pair + 2) * C]
            at = (group * 2 + pair) * 8
            dst[at : at + 8, :] = jnp.where(low, one, pltpu.roll(two, 4, 0)).astype(dst.dtype)
            dst[HALF + at : HALF + at + 8, :] = jnp.where(low, pltpu.roll(one, 4, 0), two).astype(dst.dtype)


def fold(value, dst):
    low = iota((WIN, C), 0) < 4
    for group in range(16):
        parts = []
        for pair in range(2):
            at = (group * 2 + pair) * 8
            upper = value[at : at + 8]
            lower = value[HALF + at : HALF + at + 8]
            parts.append(jnp.where(low, upper, pltpu.roll(lower, 4, 0)))
            parts.append(jnp.where(low, pltpu.roll(upper, 4, 0), lower))
        dst[:, group * 4 * C : (group + 1) * 4 * C] = jnp.concatenate(parts, axis=1).astype(dst.dtype)


def rel_slots():
    entry = iota((RELS, SLOTS), 0)
    slot = iota((RELS, SLOTS), 1)
    return ((entry // 15 == slot % 16) & (entry % 15 == slot // 16)).astype(F32)


def spread_queries():
    query = iota((HEADS * TOKENS, HEADS * 128), 0)
    place = iota((HEADS * TOKENS, HEADS * 128), 1)
    inside = query % TOKENS
    row = (inside // 32) * 4 + inside % 4
    column = (inside % 32) // 4
    return ((query // TOKENS) * 128 + column * 16 + row == place).astype(F32)


def build_bias(table, bias):
    slots = dot_split(table, rel_slots().astype(BF16))
    sub = iota((8, SLOTS), 0)
    heads = []
    for h in range(HEADS):
        line = jnp.broadcast_to(slots[h : h + 1], (8, SLOTS))
        skew = line
        for s in range(1, 8):
            skew = jnp.where(sub == s, pltpu.roll(line, 16 * (s // 4) + s % 4, 1), skew)
        groups = []
        for g in range(8):
            turn = SLOTS - 119 + 32 * (g % 4) + 4 * (g // 4)
            groups.append(pltpu.roll(skew, turn % SLOTS, 1)[:, :128])
        heads.append(jnp.concatenate(groups, axis=0))
    wide = jnp.concatenate(heads, axis=1)
    back = spread_queries().astype(BF16)
    high = wide.astype(BF16)
    rest = wide - high.astype(F32)
    middle = rest.astype(BF16)
    low = (rest - middle.astype(F32)).astype(BF16)
    bias[...] = dot(high, back, (1, 1)) + dot(middle, back, (1, 1)) + dot(low, back, (1, 1))


def table_slots(total):
    wide = dot(total.astype(BF16), spread_queries().astype(BF16))
    sub = iota((8, SLOTS), 0)
    blank = jnp.zeros((8, 128), F32)
    lines = []
    for h in range(HEADS):
        skew = jnp.zeros((8, SLOTS), F32)
        for g in range(8):
            part = jnp.concatenate([wide[8 * g : 8 * g + 8, 128 * h : 128 * h + 128], blank], axis=1)
            skew = skew + pltpu.roll(part, 119 - 32 * (g % 4) - 4 * (g // 4), 1)
        line = skew
        for s in range(1, 8):
            line = jnp.where(sub == s, pltpu.roll(skew, SLOTS - 16 * (s // 4) - s % 4, 1), line)
        lines.append(jnp.sum(line, axis=0, keepdims=True))
    return lines


def forward(x, weights, saved, blocked):
    (wq, wk, wv), wproj, wup, wdown, gamma, beta = weights
    hat, scale = normalise(x)
    saved.hat1[...] = hat
    saved.scale1[...] = scale
    normed = hat.astype(BF16)
    saved.query[...] = dot(normed, wq).astype(BF16)
    saved.key[...] = dot(normed, wk).astype(BF16)
    saved.value[...] = dot(normed, wv).astype(BF16)
    bias = saved.bias[...]
    for w in range(WINDOWS):
        query = stack_heads(window(saved.query, w))
        score = dot(window(saved.key, w), query, (1, 1)) * (HEAD**-0.5) + bias
        if blocked is not None:
            score = jnp.where(blocked, -1e9, score)
        raised = jnp.exp(score - jnp.max(score, axis=0, keepdims=True))
        attn = raised / jnp.sum(raised, axis=0, keepdims=True)
        saved.attn[w] = attn
        mixed = merge_heads(dot(attn.astype(BF16), window(saved.value, w), (0, 0)))
        put_window(saved.mixed, w, mixed)
    hidden = x + dot(saved.mixed[...], wproj)
    hat, scale = normalise(hidden)
    saved.hat2[...] = hat
    saved.scale2[...] = scale
    up = dot(hat.astype(BF16), wup)
    square = up * up
    bent = jnp.tanh(GELU_A * up * (1.0 + GELU_B * square))
    half = 0.5 * (1.0 + bent)
    lifted = (up * half).astype(BF16)
    saved.lifted[...] = lifted
    saved.slope[...] = half + 0.5 * up * (1.0 - bent * bent) * (GELU_A * (1.0 + 3.0 * GELU_B * square))
    gdn = hidden + dot(lifted, wdown, (1, 1))
    power = beta + dot((gdn * gdn).astype(BF16), gamma)
    root = lax.rsqrt(power)
    saved.gdn[...] = gdn
    saved.root[...] = root
    return gdn * root


def backward(grad, weights, saved, pack, early=None):
    (wq, wk, wv), wproj, wup, wdown, gamma, beta = weights
    gdn = saved.gdn[...]
    root = saved.root[...]
    dpower = -0.5 * grad * gdn * (root * root * root)
    dpower_16 = dpower.astype(BF16)
    gamma_grad = dot((gdn * gdn).astype(BF16), dpower_16, (0, 0))
    for i in range(3):
        pack[576 + C * i : 576 + C * (i + 1), C:128] = gamma_grad[:, 32 * i : 32 * (i + 1)].astype(BF16)
    beta_grad = jnp.sum(dpower, axis=0, keepdims=True)
    dgdn = grad * root + 2.0 * gdn * dot(dpower_16, gamma, (1, 1))
    dgdn_16 = dgdn.astype(BF16)
    down_grad = dot(dgdn_16, saved.lifted[...], (0, 0))
    for i in range(3):
        pack[288 + C * i : 288 + C * (i + 1), :] = down_grad[:, 128 * i : 128 * (i + 1)].astype(BF16)
    dup = (dot(dgdn_16, wdown) * saved.slope[...]).astype(BF16)
    hat2 = saved.hat2[...]
    up_grad = dot(hat2.astype(BF16), dup, (0, 0))
    for i in range(3):
        pack[C * i : C * (i + 1), :] = up_grad[:, 128 * i : 128 * (i + 1)].astype(BF16)
    dhidden = dgdn + norm_back(dot(dup, wup, (1, 1)), hat2, saved.scale2[...])
    dhidden_16 = dhidden.astype(BF16)
    proj_grad = dot(saved.mixed[...], dhidden_16, (0, 0))
    pack[864:960, 0:C] = proj_grad.astype(BF16)
    saved.dmixed[...] = dot(dhidden_16, wproj, (1, 1)).astype(BF16)
    if early is not None:
        early()
    total = jnp.zeros((TOKENS, HEADS * TOKENS), F32)
    for w in range(WINDOWS):
        dmixed = stack_heads(window(saved.dmixed, w))
        attn = saved.attn[w]
        dattn = dot(window(saved.value, w), dmixed, (1, 1))
        put_window(saved.dvalue, w, dot(attn.astype(BF16), dmixed))
        dscore = attn * (dattn - jnp.sum(attn * dattn, axis=0, keepdims=True))
        total = total + dscore
        dscore = (dscore * (HEAD**-0.5)).astype(BF16)
        put_window(saved.dkey, w, dot(dscore, stack_heads(window(saved.query, w))))
        put_window(saved.dquery, w, merge_heads(dot(dscore, window(saved.key, w), (0, 0))))
    lines = table_slots(total)
    hat1 = saved.hat1[...]
    normed = hat1.astype(BF16)
    dnormed = jnp.zeros((PIX, C), F32)
    for i, (part, weight) in enumerate(((saved.dquery, wq), (saved.dkey, wk), (saved.dvalue, wv))):
        piece = part[...]
        pack[576 + C * i : 576 + C * (i + 1), 0:C] = dot(normed, piece, (0, 0)).astype(BF16)
        dnormed = dnormed + dot(piece, weight, (1, 1))
    edge = jnp.concatenate([beta_grad, jnp.zeros((1, 128 - C), F32)], axis=1)
    rows = [edge] + [line[:, 128 * i : 128 * (i + 1)] for line in lines for i in range(2)]
    rows.append(jnp.zeros((ROWS - 967, 128), F32))
    pack[960:ROWS, :] = jnp.concatenate(rows, axis=0).astype(BF16)
    return dhidden + norm_back(dnormed, hat1, saved.scale1[...])


class Saved:
    names = {
        "hat1": ((PIX, C), F32),
        "scale1": ((PIX, 1), F32),
        "query": ((PIX, C), BF16),
        "key": ((PIX, C), BF16),
        "value": ((PIX, C), BF16),
        "bias": ((TOKENS, HEADS * TOKENS), F32),
        "attn": ((WINDOWS, TOKENS, HEADS * TOKENS), F32),
        "mixed": ((PIX, C), BF16),
        "hat2": ((PIX, C), F32),
        "scale2": ((PIX, 1), F32),
        "lifted": ((PIX, HID), BF16),
        "slope": ((PIX, HID), F32),
        "gdn": ((PIX, C), F32),
        "root": ((PIX, C), F32),
        "dmixed": ((PIX, C), BF16),
        "dquery": ((PIX, C), BF16),
        "dkey": ((PIX, C), BF16),
        "dvalue": ((PIX, C), BF16),
    }

    def __init__(self, refs):
        for name, ref in zip(Saved.names, refs):
            setattr(self, name, ref)


def copy_to(src, dst, send, recv, device):
    return pltpu.make_async_remote_copy(
        src_ref=src, dst_ref=dst, send_sem=send, recv_sem=recv, device_id=device, device_id_type=MESH
    )


def read_weights(b, refs):
    wqkv, wproj, wup, wdown, gamma, beta = refs
    whole = wqkv[b].astype(F32)
    parts = tuple(whole[:, C * i : C * (i + 1)].astype(BF16) for i in range(3))
    return parts, wproj[b], wup[b], wdown[b], gamma[b].astype(BF16), beta[b : b + 1, :]


class Exchange:
    def __init__(self, n_lat, n_lon, base, pack, total, first, planes, sems):
        self.n_lat, self.planes_n, self.size = n_lat, n_lon // QUAD, n_lat * QUAD
        self.base, self.pack, self.total = base, pack, total
        self.first, self.planes, self.sems = first, planes, sems
        self.rows = first.shape[1]
        self.lat, lon = lax.axis_index("lat"), lax.axis_index("lon")
        self.quad, self.z = lax.rem(lon, QUAD), lon // QUAD
        self.place = self.lat * QUAD + self.quad

    def piece(self, ref, i):
        return ref.at[pl.ds(pl.multiple_of(self.base + i * self.rows, UNIT), self.rows), :]

    def in_plane(self, make):
        def body(i, _):
            step = lax.rem(4 * i + 1, 7) + 1 if self.n_lat == 8 else i + 1
            for turn in (2, 1, 3, 0):
                make(step, turn).start()
            return 0

        lax.fori_loop(0, self.n_lat - 1, body, 0)
        for turn in (2, 1, 3):
            make(0, turn).start()

    def target(self, step, turn):
        lat = lax.rem(self.lat + step, self.n_lat)
        quad = lax.rem(self.quad + turn, QUAD)
        return lat * QUAD + quad, (lat, self.z * QUAD + quad)

    def scatter_copy(self, step, turn):
        place, device = self.target(step, turn)
        slot = self.first.at[step * QUAD + turn]
        return copy_to(self.piece(self.pack, place), slot, self.sems.at[0], self.sems.at[1], device)

    def gather_copy(self, step, turn):
        _, device = self.target(step, turn)
        mine = self.piece(self.total, self.place)
        return copy_to(mine, mine, self.sems.at[4], self.sems.at[5], device)

    def plane_copy(self, step):
        z = lax.rem(self.z + step, self.planes_n)
        slot = self.planes.at[self.z]
        device = (self.lat, z * QUAD + self.quad)
        return copy_to(slot, slot, self.sems.at[2], self.sems.at[3], device)

    def wait_both(self, ref, sem):
        for i in range(2):
            pltpu.make_async_copy(ref, ref, self.sems.at[sem + i]).wait()

    def start(self):
        self.in_plane(self.scatter_copy)

    def add_plane(self):
        self.wait_both(self.first.at[pl.ds(1, self.size - 1)], 0)
        total = self.piece(self.pack, self.place)[...].astype(F32)
        for i in range(1, self.size):
            total = total + self.first[i].astype(F32)
        self.planes[self.z] = total.astype(BF16)

        def body(step, _):
            self.plane_copy(step).start()
            return 0

        lax.fori_loop(1, self.planes_n, body, 0)

    def add_all(self, factor):
        if self.planes_n > 1:
            self.wait_both(self.planes.at[pl.ds(0, self.planes_n - 1)], 2)
        total = self.planes[0].astype(F32)
        for i in range(1, self.planes_n):
            total = total + self.planes[i].astype(F32)
        self.piece(self.total, self.place)[...] = (total * factor).astype(BF16)
        self.in_plane(self.gather_copy)

    def finish(self):
        self.wait_both(self.total.at[pl.ds(self.base, (self.size - 1) * self.rows), :], 4)


def exchange_scratch(n_lat, n_lon, rows):
    rows = rows // (n_lat * QUAD)
    return [
        pltpu.VMEM((n_lat * QUAD, rows, 128), BF16),
        pltpu.VMEM((n_lon // QUAD, rows, 128), BF16),
        pltpu.SemaphoreType.DMA((6,)),
    ]


def unpack(b, total, outs):
    qkv, proj, up, down, gamma, beta, table = outs
    first = total[576:864, :].astype(F32)
    parts = [first[C * i : C * (i + 1)] for i in range(3)]
    qkv[b] = jnp.concatenate([part[:, 0:C] for part in parts], axis=1)
    gamma[b] = jnp.concatenate([part[:, C:128] for part in parts], axis=1)
    proj[b] = total[864:960, 0:C].astype(F32)
    for i in range(3):
        up[b, :, 128 * i : 128 * (i + 1)] = total[C * i : C * (i + 1), :].astype(F32)
        down[b, :, 128 * i : 128 * (i + 1)] = total[288 + C * i : 288 + C * (i + 1), :].astype(F32)
    edge = total[960:976, :].astype(F32)
    beta[b : b + 1, :] = edge[0:1, 0:C]
    lines = [jnp.concatenate([edge[1 + 2 * h : 2 + 2 * h], edge[2 + 2 * h : 3 + 2 * h]], axis=1) for h in range(HEADS)]
    slots = jnp.concatenate(lines, axis=0).astype(BF16)
    table[:, b, :] = dot(slots, rel_slots().astype(BF16), (1, 1))


def unpack_kernel(*refs):
    ins, outs, staged, held, sems = refs[:4], refs[4:13], refs[13:20], refs[20:24], refs[24]
    loads = [pltpu.make_async_copy(src, dst, sems.at[9 + i]) for i, (src, dst) in enumerate(zip(ins, held))]
    sources = tuple(held[:2]) + tuple(staged)
    copies = [pltpu.make_async_copy(src, dst, sems.at[i]) for i, (src, dst) in enumerate(zip(sources, outs))]
    for i in (2, 3, 0, 1):
        loads[i].start()
    for b in range(2):
        loads[2 + b].wait()
        unpack(b, held[2 + b], staged)
    for i in range(2):
        loads[i].wait()
    for copy in copies:
        copy.start()
    for copy in copies:
        copy.wait()


def kernel(n_lat, n_lon, *refs):
    refs = list(refs)

    def take(count):
        taken = refs[:count]
        del refs[:count]
        return taken

    hbm_args = take(9)
    results = take(4)
    args = take(9)
    (arg_sems,) = take(1)
    saved = [Saved(take(len(Saved.names))) for _ in range(2)]
    field, send_out, send_cot, send_dec, send_grad = take(5)
    south, east, corner, halo_send, halo_recv = take(5)
    packs, fields, totals = take(2), take(2), take(2)
    (result_sems,) = take(1)
    whole = Exchange(n_lat, n_lon, 0, packs[1], totals[1], *take(3))
    upper = Exchange(n_lat, n_lon, 0, packs[0], totals[0], *take(3))
    lower = Exchange(n_lat, n_lon, ROWS // 2, packs[0], totals[0], *take(3))
    lat, lon = lax.axis_index("lat"), lax.axis_index("lon")
    above, below = lax.rem(lat + n_lat - 1, n_lat), lax.rem(lat + 1, n_lat)
    west, easterly = lax.rem(lon + n_lon - 1, n_lon), lax.rem(lon + 1, n_lon)

    stores = [
        pltpu.make_async_copy(src, dst, result_sems.at[i]) for i, (src, dst) in enumerate(zip(fields + totals, results))
    ]
    loads = [pltpu.make_async_copy(src, dst, arg_sems.at[i]) for i, (src, dst) in enumerate(zip(hbm_args, args))]
    for load in loads:
        load.start()
    barrier = pltpu.get_barrier_semaphore()

    def greet(device):
        pl.semaphore_signal(barrier, inc=1, device_id=device, device_id_type=MESH)

    def greet_plane(i, _):
        _, device = whole.target(i // QUAD, lax.rem(i, QUAD))
        greet(device)
        return 0

    def greet_planes(i, _):
        greet((lat, lax.rem(lon + QUAD * i, n_lon)))
        return 0

    planes_n = n_lon // QUAD
    lax.fori_loop(1, n_lat * QUAD, greet_plane, 0)
    lax.fori_loop(1, planes_n, greet_planes, 0)
    for device in ((lat, west), (lat, easterly), (above, west), (below, easterly)):
        greet(device)
    greetings = n_lat * QUAD + planes_n + 2

    def halo(i, ref, rows, devices):
        copies = []
        for j, target in enumerate((south, east, corner)):
            src = ref.at[pl.ds(rows[j][0], rows[j][1]), :]
            k = 3 * i + j
            copies.append(copy_to(src, target.at[i], halo_send.at[k], halo_recv.at[k], devices[j]))
        return copies

    def up_halo(i, ref):
        rows = ((0, HALF), (HALF, UNIT), (0, UNIT))
        return halo(i, ref, rows, ((above, lon), (lat, west), (above, west)))

    def down_halo(i, ref):
        rows = ((HALF, HALF), (HALF - UNIT, UNIT), (PIX - UNIT, UNIT))
        return halo(i, ref, rows, ((below, lon), (lat, easterly), (below, easterly)))

    def shifted(i, ref):
        parts = [ref[HALF + UNIT : PIX, :], east[i], south[i, UNIT:HALF, :], corner[i]]
        return jnp.concatenate([part.astype(F32) for part in parts], axis=0)

    def unshifted(i, ref):
        parts = [corner[i], south[i, 0 : HALF - UNIT, :], east[i], ref[0 : HALF - UNIT, :]]
        return jnp.concatenate([part.astype(F32) for part in parts], axis=0)

    for load in loads:
        load.wait()
    sig, cot, table = args[0], args[1], args[8]
    unfold(sig, field)
    build_bias(table[:, 0, :], saved[0].bias)
    weights = [read_weights(b, args[2:8]) for b in range(2)]
    output = forward(field[...], weights[0], saved[0], None)
    send_out[...] = output.astype(BF16)

    pl.semaphore_wait(barrier, greetings)
    out_copies = up_halo(0, send_out)
    for copy in out_copies:
        copy.start()
    unfold(cot, send_cot)
    cot_copies = up_halo(1, send_cot)
    for copy in cot_copies:
        copy.start()
    build_bias(table[:, 1, :], saved[1].bias)
    for copy in out_copies:
        copy.wait()
    is_last = (lat == n_lat - 1).astype(jnp.int32)
    shape = (TOKENS, HEADS * TOKENS)
    differ = (iota(shape, 0) // 32 != (iota(shape, 1) % TOKENS) // 32).astype(jnp.int32)
    blocked = differ * is_last > 0
    output = forward(shifted(0, send_out), weights[1], saved[1], blocked)
    send_dec[...] = output.astype(BF16)
    dec_copies = down_halo(2, send_dec)
    for copy in dec_copies:
        copy.start()
    for copy in cot_copies:
        copy.wait()
    back = backward(shifted(1, send_cot), weights[1], saved[1], packs[1])
    send_grad[...] = back.astype(BF16)
    grad_copies = down_halo(3, send_grad)
    for copy in grad_copies:
        copy.start()
    whole.start()
    for copy in dec_copies:
        copy.wait()
    fold(unshifted(2, send_dec), fields[0])
    stores[0].start()
    for copy in grad_copies:
        copy.wait()
    factor = 1.0 / math.sqrt(PIX * n_lat * n_lon)

    back = backward(unshifted(3, send_grad), weights[0], saved[0], packs[0], upper.start)
    lower.start()
    fold(back, fields[1])
    stores[1].start()
    whole.add_plane()
    upper.add_plane()
    lower.add_plane()
    whole.add_all(factor)
    upper.add_all(factor)
    lower.add_all(factor)
    whole.finish()
    stores[3].start()
    upper.finish()
    lower.finish()
    stores[2].start()
    for store in stores:
        store.wait()


def solution(mesh):
    n_lat, n_lon = mesh.shape["lat"], mesh.shape["lon"]

    def per_device(sig, cot, wqkv, wproj, wup, wdown, gamma, beta, table):
        dma = pltpu.SemaphoreType.DMA
        args = (sig, cot, wqkv, wproj, wup, jnp.swapaxes(wdown, 1, 2), gamma, beta, jnp.swapaxes(table, 0, 1))
        saved = [pltpu.VMEM(shape, kind) for shape, kind in Saved.names.values()]
        scratch = [pltpu.VMEM(arg.shape, arg.dtype) for arg in args] + [dma((9,))]
        scratch += saved + saved
        scratch += [pltpu.VMEM((PIX, C), F32)] + [pltpu.VMEM((PIX, C), BF16)] * 4
        scratch += [
            pltpu.VMEM((4, HALF, C), BF16),
            pltpu.VMEM((4, UNIT, C), BF16),
            pltpu.VMEM((4, UNIT, C), BF16),
            dma((12,)),
            dma((12,)),
        ]
        scratch += [pltpu.VMEM((ROWS, 128), BF16)] * 2 + [pltpu.VMEM(sig.shape, BF16)] * 2
        scratch += [pltpu.VMEM((ROWS, 128), BF16)] * 2 + [dma((4,))]
        scratch += exchange_scratch(n_lat, n_lon, ROWS)
        scratch += exchange_scratch(n_lat, n_lon, ROWS // 2) * 2
        hbm = pl.BlockSpec(memory_space=pltpu.HBM)
        field = jax.ShapeDtypeStruct(sig.shape, BF16)
        total = jax.ShapeDtypeStruct((ROWS, 128), BF16)
        results = pl.pallas_call(
            functools.partial(kernel, n_lat, n_lon),
            out_shape=[field, field, total, total],
            in_specs=[hbm] * 9,
            out_specs=[hbm] * 4,
            scratch_shapes=scratch,
            compiler_params=pltpu.CompilerParams(
                collective_id=0, has_side_effects=True, vmem_limit_bytes=62 * 1024 * 1024
            ),
        )(*args)
        grads = [jax.ShapeDtypeStruct(leaf.shape, F32) for leaf in args[2:]]
        outs = pl.pallas_call(
            unpack_kernel,
            out_shape=[field, field] + grads,
            in_specs=[hbm] * 4,
            out_specs=[hbm] * 9,
            scratch_shapes=[pltpu.VMEM(leaf.shape, F32) for leaf in args[2:]]
            + [pltpu.VMEM(sig.shape, BF16)] * 2
            + [pltpu.VMEM((ROWS, 128), BF16)] * 2
            + [dma((13,))],
            compiler_params=pltpu.CompilerParams(vmem_limit_bytes=62 * 1024 * 1024),
        )(*results)
        decoded, sgrad, qkv, proj, up, down, gammas, betas, tables = outs
        return decoded, sgrad, qkv, proj, up, jnp.swapaxes(down, 1, 2), gammas, betas, jnp.swapaxes(tables, 0, 1)

    in_specs = (P("lat", "lon"), P("lat", "lon"), P(), P(), P(), P(), P(), P(), P())
    out_specs = (P("lat", "lon"), P("lat", "lon"), P(), P(), P(), P(), P(), P(), P())
    return jax.shard_map(per_device, mesh=mesh, in_specs=in_specs, out_specs=out_specs, check_vma=False)
```

```python
import functools
import math

import jax
import jax.numpy as jnp
from jax import lax
from jax.experimental import pallas as pl
from jax.experimental.pallas import tpu as pltpu
from jax.sharding import PartitionSpec as P

C = 96
HEADS = 3
HEAD = 32
HID = 384
WIN = 8
RELS = 225
SLOTS = 256
PIX = 512
HALF = 256
UNIT = 16
WINDOWS = 8
TOKENS = 64
ROWS = 1024
QUAD = 4
EPS = 1e-05
GELU_A = math.sqrt(2.0 / math.pi)
GELU_B = 0.044715
MESH = pl.DeviceIdType.MESH
F32 = jnp.float32
BF16 = jnp.bfloat16


def iota(shape, dim):
    return lax.broadcasted_iota(jnp.int32, shape, dim)


def dot(a, b, over=(1, 0)):
    return lax.dot_general(a, b, (((over[0],), (over[1],)), ((), ())), preferred_element_type=F32)


def dot_split(a, b):
    high = a.astype(BF16)
    rest = a - high.astype(F32)
    middle = rest.astype(BF16)
    low = (rest - middle.astype(F32)).astype(BF16)
    return dot(high, b) + dot(middle, b) + dot(low, b)


def row_mean(a):
    return jnp.sum(a, axis=-1, keepdims=True) * (1.0 / C)


def normalise(v):
    center = v - row_mean(v)
    scale = lax.rsqrt(row_mean(center * center) + EPS)
    return center * scale, scale


def norm_back(grad, hat, scale):
    return scale * (grad - row_mean(grad) - hat * row_mean(grad * hat))


def stack_heads(a):
    head_of = iota(a.shape, 1) // HEAD
    zero = jnp.zeros_like(a)
    return jnp.concatenate([jnp.where(head_of == h, a, zero) for h in range(HEADS)], axis=0)


def merge_heads(a):
    parts = [a[h * TOKENS : (h + 1) * TOKENS] for h in range(HEADS)]
    head_of = iota((TOKENS, C), 1) // HEAD
    return jnp.where(head_of == 0, parts[0], jnp.where(head_of == 1, parts[1], parts[2]))


def window(ref, w):
    step = TOKENS // 2
    upper = ref[w * step : (w + 1) * step, :]
    lower = ref[HALF + w * step : HALF + (w + 1) * step, :]
    return jnp.concatenate([upper, lower], axis=0)


def put_window(ref, w, value):
    step = TOKENS // 2
    ref[w * step : (w + 1) * step, :] = value[:step].astype(ref.dtype)
    ref[HALF + w * step : HALF + (w + 1) * step, :] = value[step:].astype(ref.dtype)


def unfold(src, dst):
    low = iota((WIN, C), 0) < 4
    for group in range(16):
        part = src[:, group * 4 * C : (group + 1) * 4 * C].astype(F32)
        for pair in range(2):
            one = part[:, (2 * pair) * C : (2 * pair + 1) * C]
            two = part[:, (2 * pair + 1) * C : (2 * pair + 2) * C]
            at = (group * 2 + pair) * 8
            dst[at : at + 8, :] = jnp.where(low, one, pltpu.roll(two, 4, 0)).astype(dst.dtype)
            dst[HALF + at : HALF + at + 8, :] = jnp.where(low, pltpu.roll(one, 4, 0), two).astype(dst.dtype)


def fold(value, dst):
    low = iota((WIN, C), 0) < 4
    for group in range(16):
        parts = []
        for pair in range(2):
            at = (group * 2 + pair) * 8
            upper = value[at : at + 8]
            lower = value[HALF + at : HALF + at + 8]
            parts.append(jnp.where(low, upper, pltpu.roll(lower, 4, 0)))
            parts.append(jnp.where(low, pltpu.roll(upper, 4, 0), lower))
        dst[:, group * 4 * C : (group + 1) * 4 * C] = jnp.concatenate(parts, axis=1).astype(dst.dtype)


def rel_slots():
    entry = iota((RELS, SLOTS), 0)
    slot = iota((RELS, SLOTS), 1)
    return ((entry // 15 == slot % 16) & (entry % 15 == slot // 16)).astype(F32)


def spread_queries():
    query = iota((HEADS * TOKENS, HEADS * 128), 0)
    place = iota((HEADS * TOKENS, HEADS * 128), 1)
    inside = query % TOKENS
    row = (inside // 32) * 4 + inside % 4
    column = (inside % 32) // 4
    return ((query // TOKENS) * 128 + column * 16 + row == place).astype(F32)


def build_bias(table, slot_ref, spread_ref, bias):
    slots = dot_split(table, slot_ref[...])
    sub = iota((8, SLOTS), 0)
    heads = []
    for h in range(HEADS):
        line = jnp.broadcast_to(slots[h : h + 1], (8, SLOTS))
        skew = line
        for s in range(1, 8):
            skew = jnp.where(sub == s, pltpu.roll(line, 16 * (s // 4) + s % 4, 1), skew)
        groups = []
        for g in range(8):
            turn = SLOTS - 119 + 32 * (g % 4) + 4 * (g // 4)
            groups.append(pltpu.roll(skew, turn % SLOTS, 1)[:, :128])
        heads.append(jnp.concatenate(groups, axis=0))
    wide = jnp.concatenate(heads, axis=1)
    back = spread_ref[...]
    high = wide.astype(BF16)
    rest = wide - high.astype(F32)
    middle = rest.astype(BF16)
    low = (rest - middle.astype(F32)).astype(BF16)
    bias[...] = dot(high, back, (1, 1)) + dot(middle, back, (1, 1)) + dot(low, back, (1, 1))


def table_slots(total, spread_ref):
    wide = dot(total.astype(BF16), spread_ref[...])
    sub = iota((8, SLOTS), 0)
    blank = jnp.zeros((8, 128), F32)
    lines = []
    for h in range(HEADS):
        skew = jnp.zeros((8, SLOTS), F32)
        for g in range(8):
            part = jnp.concatenate([wide[8 * g : 8 * g + 8, 128 * h : 128 * h + 128], blank], axis=1)
            skew = skew + pltpu.roll(part, 119 - 32 * (g % 4) - 4 * (g // 4), 1)
        line = skew
        for s in range(1, 8):
            line = jnp.where(sub == s, pltpu.roll(skew, SLOTS - 16 * (s // 4) - s % 4, 1), line)
        lines.append(jnp.sum(line, axis=0, keepdims=True))
    return lines


def gelu_parts(up):
    square = up * up
    bent = jnp.tanh(GELU_A * up * (1.0 + GELU_B * square))
    return square, bent, 0.5 * (1.0 + bent)


def gelu_slope(up, square, bent, half):
    return half + 0.5 * up * (1.0 - bent * bent) * (GELU_A * (1.0 + 3.0 * GELU_B * square))


def project(x, weights, saved, start):
    rows = slice(start, start + x.shape[0])
    wq, wk, wv = weights[0]
    hat, scale = normalise(x)
    saved.hat1[rows, :] = hat
    saved.scale1[rows, :] = scale
    normed = hat.astype(BF16)
    saved.query[rows, :] = dot(normed, wq).astype(BF16)
    saved.key[rows, :] = dot(normed, wk).astype(BF16)
    saved.value[rows, :] = dot(normed, wv).astype(BF16)


def forward(x, weights, saved, blocked, slope_later):
    _, wproj, wup, wdown, gamma, beta = weights
    bias = saved.bias[...]
    every = range(WINDOWS)
    scores = [dot(window(saved.key, w), stack_heads(window(saved.query, w)), (1, 1)) for w in every]
    scores = [score * (HEAD**-0.5) + bias for score in scores]
    if blocked is not None:
        scores = [jnp.where(blocked, -1e9, score) for score in scores]
    scores = [jnp.exp(score - jnp.max(score, axis=0, keepdims=True)) for score in scores]
    attns = [score / jnp.sum(score, axis=0, keepdims=True) for score in scores]
    for w in every:
        saved.attn[w] = attns[w]
    mixed = [dot(attns[w].astype(BF16), window(saved.value, w), (0, 0)) for w in every]
    for w in every:
        put_window(saved.mixed, w, merge_heads(mixed[w]))
    hidden = x + dot(saved.mixed[...], wproj)
    hat, scale = normalise(hidden)
    saved.hat2[...] = hat
    saved.scale2[...] = scale
    up = dot(hat.astype(BF16), wup)
    square, bent, half = gelu_parts(up)
    lifted = (up * half).astype(BF16)
    saved.lifted[...] = lifted
    saved.slope[...] = up if slope_later else gelu_slope(up, square, bent, half)
    gdn = hidden + dot(lifted, wdown, (1, 1))
    power = beta + dot((gdn * gdn).astype(BF16), gamma)
    root = lax.rsqrt(power)
    saved.gdn[...] = gdn
    saved.root[...] = root
    return gdn * root


def prepare(saved):
    up = saved.slope[...]
    saved.slope[...] = gelu_slope(up, *gelu_parts(up))


def transpose_saved(saved):
    saved.normed_t[...] = saved.hat1[...].T.astype(BF16)
    saved.hat2_t[...] = saved.hat2[...].T.astype(BF16)
    saved.mixed_t[...] = saved.mixed[...].astype(F32).T.astype(BF16)
    gdn = saved.gdn[...]
    saved.square_t[...] = (gdn * gdn).T.astype(BF16)


def back_mlp(grad, weights, saved, start):
    rows = slice(start, start + grad.shape[0])
    _, wproj, wup, wdown, gamma, _ = weights
    gdn = saved.gdn[rows, :]
    root = saved.root[rows, :]
    dpower = -0.5 * grad * gdn * (root * root * root)
    dpower_16 = dpower.astype(BF16)
    saved.dpower[rows, :] = dpower_16
    dgdn = grad * root + 2.0 * gdn * dot(dpower_16, gamma, (1, 1))
    dgdn_16 = dgdn.astype(BF16)
    saved.dgdn[rows, :] = dgdn_16
    dup = (dot(dgdn_16, wdown) * saved.slope[rows, :]).astype(BF16)
    saved.dup[rows, :] = dup
    dhidden = dgdn + norm_back(dot(dup, wup, (1, 1)), saved.hat2[rows, :], saved.scale2[rows, :])
    dhidden_16 = dhidden.astype(BF16)
    saved.dhidden[rows, :] = dhidden_16
    saved.dmixed[rows, :] = dot(dhidden_16, wproj, (1, 1)).astype(BF16)
    saved.wide[rows, :] = dhidden
    return jnp.sum(dpower, axis=0, keepdims=True)


def grads_mlp(saved, pack):
    down_grad = dot(saved.dgdn[...], saved.lifted[...], (0, 0))
    up_grad = dot(saved.hat2_t[...], saved.dup[...])
    gamma_grad = dot(saved.square_t[...], saved.dpower[...])
    for i in range(3):
        pack[C * i : C * (i + 1), :] = up_grad[:, 128 * i : 128 * (i + 1)].astype(BF16)
        pack[288 + C * i : 288 + C * (i + 1), :] = down_grad[:, 128 * i : 128 * (i + 1)].astype(BF16)
        pack[576 + C * i : 576 + C * (i + 1), C:128] = gamma_grad[:, 32 * i : 32 * (i + 1)].astype(BF16)
    pack[864:960, 0:C] = dot(saved.mixed_t[...], saved.dhidden[...]).astype(BF16)


def back_attention(saved):
    every = range(WINDOWS)
    dmixed = [stack_heads(window(saved.dmixed, w)) for w in every]
    dattns = [dot(window(saved.value, w), dmixed[w], (1, 1)) for w in every]
    dvalues = [dot(saved.attn[w].astype(BF16), dmixed[w]) for w in every]
    for w in every:
        put_window(saved.dvalue, w, dvalues[w])
    dscores = []
    for w in every:
        attn = saved.attn[w]
        dscores.append(attn * (dattns[w] - jnp.sum(attn * dattns[w], axis=0, keepdims=True)))
    total = dscores[0]
    for w in every[1:]:
        total = total + dscores[w]
    dscores = [(dscore * (HEAD**-0.5)).astype(BF16) for dscore in dscores]
    dqueries = [dot(dscores[w], window(saved.key, w), (0, 0)) for w in every]
    dkeys = [dot(dscores[w], stack_heads(window(saved.query, w))) for w in every]
    for w in every:
        put_window(saved.dkey, w, dkeys[w])
        put_window(saved.dquery, w, merge_heads(dqueries[w]))
    return total


def grads_attention(saved, pack, total, beta_grad, spread_ref):
    for i, part in enumerate((saved.dquery, saved.dkey, saved.dvalue)):
        pack[576 + C * i : 576 + C * (i + 1), 0:C] = dot(saved.normed_t[...], part[...]).astype(BF16)
    edge = jnp.concatenate([beta_grad, jnp.zeros((1, 128 - C), F32)], axis=1)
    lines = table_slots(total, spread_ref)
    rows = [edge] + [line[:, 128 * i : 128 * (i + 1)] for line in lines for i in range(2)]
    rows.append(jnp.zeros((ROWS - 967, 128), F32))
    pack[960:ROWS, :] = jnp.concatenate(rows, axis=0).astype(BF16)


def back_input(weights, saved):
    wq, wk, wv = weights[0]
    dnormed = dot(saved.dquery[...], wq, (1, 1)) + dot(saved.dkey[...], wk, (1, 1)) + dot(saved.dvalue[...], wv, (1, 1))
    return saved.wide[...] + norm_back(dnormed, saved.hat1[...], saved.scale1[...])


class Saved:
    names = {
        "hat1": ((PIX, C), F32),
        "scale1": ((PIX, 1), F32),
        "query": ((PIX, C), BF16),
        "key": ((PIX, C), BF16),
        "value": ((PIX, C), BF16),
        "bias": ((TOKENS, HEADS * TOKENS), F32),
        "attn": ((WINDOWS, TOKENS, HEADS * TOKENS), F32),
        "mixed": ((PIX, C), BF16),
        "hat2": ((PIX, C), F32),
        "scale2": ((PIX, 1), F32),
        "lifted": ((PIX, HID), BF16),
        "slope": ((PIX, HID), F32),
        "gdn": ((PIX, C), F32),
        "root": ((PIX, C), F32),
        "dmixed": ((PIX, C), BF16),
        "dquery": ((PIX, C), BF16),
        "dkey": ((PIX, C), BF16),
        "dvalue": ((PIX, C), BF16),
        "dpower": ((PIX, C), BF16),
        "dgdn": ((PIX, C), BF16),
        "dup": ((PIX, HID), BF16),
        "dhidden": ((PIX, C), BF16),
        "wide": ((PIX, C), F32),
        "normed_t": ((C, PIX), BF16),
        "hat2_t": ((C, PIX), BF16),
        "mixed_t": ((C, PIX), BF16),
        "square_t": ((C, PIX), BF16),
    }

    def __init__(self, refs):
        for name, ref in zip(Saved.names, refs):
            setattr(self, name, ref)


def copy_to(src, dst, send, recv, device):
    return pltpu.make_async_remote_copy(
        src_ref=src, dst_ref=dst, send_sem=send, recv_sem=recv, device_id=device, device_id_type=MESH
    )


def read_weights(b, refs):
    wqkv, wproj, wup, wdown, gamma, beta = refs
    whole = wqkv[b].astype(F32)
    parts = tuple(whole[:, C * i : C * (i + 1)].astype(BF16) for i in range(3))
    return parts, wproj[b], wup[b], wdown[b], gamma[b].astype(BF16), beta[b : b + 1, :]


class Exchange:
    def __init__(self, n_lat, n_lon, base, pack, total, first, planes, sems):
        self.n_lat, self.planes_n, self.size = n_lat, n_lon // QUAD, n_lat * QUAD
        self.base, self.pack, self.total = base, pack, total
        self.first, self.planes, self.sems = first, planes, sems
        self.rows = first.shape[1]
        self.lat, lon = lax.axis_index("lat"), lax.axis_index("lon")
        self.quad, self.z = lax.rem(lon, QUAD), lon // QUAD
        self.place = self.lat * QUAD + self.quad

    def piece(self, ref, i):
        return ref.at[pl.ds(pl.multiple_of(self.base + i * self.rows, UNIT), self.rows), :]

    def in_plane(self, make):
        def body(i, _):
            step = lax.rem(4 * i + 1, 7) + 1 if self.n_lat == 8 else i + 1
            for turn in (2, 1, 3, 0):
                make(step, turn).start()
            return 0

        lax.fori_loop(0, self.n_lat - 1, body, 0)
        for turn in (2, 1, 3):
            make(0, turn).start()

    def target(self, step, turn):
        lat = lax.rem(self.lat + step, self.n_lat)
        quad = lax.rem(self.quad + turn, QUAD)
        return lat * QUAD + quad, (lat, self.z * QUAD + quad)

    def scatter_copy(self, step, turn):
        place, device = self.target(step, turn)
        slot = self.first.at[step * QUAD + turn]
        return copy_to(self.piece(self.pack, place), slot, self.sems.at[0], self.sems.at[1], device)

    def gather_copy(self, step, turn):
        _, device = self.target(step, turn)
        mine = self.piece(self.total, self.place)
        return copy_to(mine, mine, self.sems.at[4], self.sems.at[5], device)

    def plane_copy(self, step):
        z = lax.rem(self.z + step, self.planes_n)
        slot = self.planes.at[self.z]
        device = (self.lat, z * QUAD + self.quad)
        return copy_to(slot, slot, self.sems.at[2], self.sems.at[3], device)

    def wait_both(self, ref, sem):
        for i in range(2):
            pltpu.make_async_copy(ref, ref, self.sems.at[sem + i]).wait()

    def start(self):
        self.in_plane(self.scatter_copy)

    def add_plane(self):
        self.wait_both(self.first.at[pl.ds(1, self.size - 1)], 0)
        total = self.piece(self.pack, self.place)[...].astype(F32)
        for i in range(1, self.size):
            total = total + self.first[i].astype(F32)
        self.planes[self.z] = total.astype(BF16)

        def body(step, _):
            self.plane_copy(step).start()
            return 0

        lax.fori_loop(1, self.planes_n, body, 0)

    def add_all(self, factor):
        if self.planes_n > 1:
            self.wait_both(self.planes.at[pl.ds(0, self.planes_n - 1)], 2)
        total = self.planes[0].astype(F32)
        for i in range(1, self.planes_n):
            total = total + self.planes[i].astype(F32)
        self.piece(self.total, self.place)[...] = (total * factor).astype(BF16)
        self.in_plane(self.gather_copy)

    def finish(self):
        self.wait_both(self.total.at[pl.ds(self.base, (self.size - 1) * self.rows), :], 4)


def exchange_scratch(n_lat, n_lon, rows):
    rows = rows // (n_lat * QUAD)
    return [
        pltpu.VMEM((n_lat * QUAD, rows, 128), BF16),
        pltpu.VMEM((n_lon // QUAD, rows, 128), BF16),
        pltpu.SemaphoreType.DMA((6,)),
    ]


def unpack(b, total, outs):
    qkv, proj, up, down, gamma, beta, table = outs
    first = total[576:864, :].astype(F32)
    parts = [first[C * i : C * (i + 1)] for i in range(3)]
    qkv[b] = jnp.concatenate([part[:, 0:C] for part in parts], axis=1)
    gamma[b] = jnp.concatenate([part[:, C:128] for part in parts], axis=1)
    proj[b] = total[864:960, 0:C].astype(F32)
    for i in range(3):
        up[b, :, 128 * i : 128 * (i + 1)] = total[C * i : C * (i + 1), :].astype(F32)
        down[b, :, 128 * i : 128 * (i + 1)] = total[288 + C * i : 288 + C * (i + 1), :].astype(F32)
    edge = total[960:976, :].astype(F32)
    beta[b : b + 1, :] = edge[0:1, 0:C]
    lines = [jnp.concatenate([edge[1 + 2 * h : 2 + 2 * h], edge[2 + 2 * h : 3 + 2 * h]], axis=1) for h in range(HEADS)]
    slots = jnp.concatenate(lines, axis=0).astype(BF16)
    table[:, b, :] = dot(slots, rel_slots().astype(BF16), (1, 1))


def unpack_kernel(*refs):
    ins, outs, staged, held, sems = refs[:4], refs[4:13], refs[13:20], refs[20:24], refs[24]
    loads = [pltpu.make_async_copy(src, dst, sems.at[9 + i]) for i, (src, dst) in enumerate(zip(ins, held))]
    sources = tuple(held[:2]) + tuple(staged)
    copies = [pltpu.make_async_copy(src, dst, sems.at[i]) for i, (src, dst) in enumerate(zip(sources, outs))]
    for i in (2, 3, 0, 1):
        loads[i].start()
    for b in range(2):
        loads[2 + b].wait()
        unpack(b, held[2 + b], staged)
    for i in range(2):
        loads[i].wait()
    for copy in copies:
        copy.start()
    for copy in copies:
        copy.wait()


def kernel(n_lat, n_lon, *refs):
    refs = list(refs)

    def take(count):
        taken = refs[:count]
        del refs[:count]
        return taken

    hbm_args = take(9)
    results = take(4)
    args = take(9)
    arg_sems, slot_ref, spread_ref = take(3)
    saved = [Saved(take(len(Saved.names))) for _ in range(2)]
    field, send_out, send_cot, send_dec, send_grad = take(5)
    south, east, corner, halo_send, halo_recv = take(5)
    packs, fields, totals = take(2), take(2), take(2)
    (result_sems,) = take(1)
    whole = Exchange(n_lat, n_lon, 0, packs[1], totals[1], *take(3))
    upper = Exchange(n_lat, n_lon, 0, packs[0], totals[0], *take(3))
    lower = Exchange(n_lat, n_lon, ROWS // 2, packs[0], totals[0], *take(3))
    lat, lon = lax.axis_index("lat"), lax.axis_index("lon")
    above, below = lax.rem(lat + n_lat - 1, n_lat), lax.rem(lat + 1, n_lat)
    west, easterly = lax.rem(lon + n_lon - 1, n_lon), lax.rem(lon + 1, n_lon)

    stores = [
        pltpu.make_async_copy(src, dst, result_sems.at[i]) for i, (src, dst) in enumerate(zip(fields + totals, results))
    ]
    loads = [pltpu.make_async_copy(src, dst, arg_sems.at[i]) for i, (src, dst) in enumerate(zip(hbm_args, args))]
    for load in loads:
        load.start()
    barrier = pltpu.get_barrier_semaphore()

    def greet(device):
        pl.semaphore_signal(barrier, inc=1, device_id=device, device_id_type=MESH)

    def greet_plane(i, _):
        _, device = whole.target(i // QUAD, lax.rem(i, QUAD))
        greet(device)
        return 0

    def greet_planes(i, _):
        greet((lat, lax.rem(lon + QUAD * i, n_lon)))
        return 0

    planes_n = n_lon // QUAD
    lax.fori_loop(1, n_lat * QUAD, greet_plane, 0)
    lax.fori_loop(1, planes_n, greet_planes, 0)
    for device in ((lat, west), (lat, easterly), (above, west), (below, easterly)):
        greet(device)
    greetings = n_lat * QUAD + planes_n + 2

    def halo(i, ref, rows, devices):
        copies = []
        for j, target in enumerate((south, east, corner)):
            src = ref.at[pl.ds(rows[j][0], rows[j][1]), :]
            k = 3 * i + j
            copies.append(copy_to(src, target.at[i], halo_send.at[k], halo_recv.at[k], devices[j]))
        return copies

    def up_halo(i, ref):
        rows = ((0, HALF), (HALF, UNIT), (0, UNIT))
        return halo(i, ref, rows, ((above, lon), (lat, west), (above, west)))

    def down_halo(i, ref):
        rows = ((HALF, HALF), (HALF - UNIT, UNIT), (PIX - UNIT, UNIT))
        return halo(i, ref, rows, ((below, lon), (lat, easterly), (below, easterly)))

    def shifted(i, ref):
        parts = [ref[HALF + UNIT : PIX, :], east[i], south[i, UNIT:HALF, :], corner[i]]
        return jnp.concatenate([part.astype(F32) for part in parts], axis=0)

    def unshifted(i, ref):
        parts = [corner[i], south[i, 0 : HALF - UNIT, :], east[i], ref[0 : HALF - UNIT, :]]
        return jnp.concatenate([part.astype(F32) for part in parts], axis=0)

    sig, cot, table = args[0], args[1], args[8]
    slot_ref[...] = rel_slots().astype(BF16)
    spread_ref[...] = spread_queries().astype(BF16)
    loads[8].wait()
    build_bias(table[:, 0, :], slot_ref, spread_ref, saved[0].bias)
    for load in loads[:8]:
        load.wait()
    unfold(sig, field)
    weights = [read_weights(b, args[2:8]) for b in range(2)]
    project(field[...], weights[0], saved[0], 0)
    output = forward(field[...], weights[0], saved[0], None, True)
    send_out[...] = output.astype(BF16)

    pl.semaphore_wait(barrier, greetings)
    out_copies = up_halo(0, send_out)
    for copy in out_copies:
        copy.start()
    unfold(cot, send_cot)
    cot_copies = up_halo(1, send_cot)
    for copy in cot_copies:
        copy.start()
    build_bias(table[:, 1, :], slot_ref, spread_ref, saved[1].bias)
    is_last = (lat == n_lat - 1).astype(jnp.int32)
    shape = (TOKENS, HEADS * TOKENS)
    differ = (iota(shape, 0) // 32 != (iota(shape, 1) % TOKENS) // 32).astype(jnp.int32)
    blocked = differ * is_last > 0
    own = HALF - UNIT
    project(send_out[HALF + UNIT : PIX, :].astype(F32), weights[1], saved[1], 0)
    prepare(saved[0])
    for copy in out_copies:
        copy.wait()
    field[...] = shifted(0, send_out)
    project(field[own:PIX, :], weights[1], saved[1], own)
    output = forward(field[...], weights[1], saved[1], blocked, False)
    send_dec[...] = output.astype(BF16)
    dec_copies = down_halo(2, send_dec)
    for copy in dec_copies:
        copy.start()
    for copy in cot_copies:
        copy.wait()
    beta_grad = back_mlp(shifted(1, send_cot), weights[1], saved[1], 0)
    total = back_attention(saved[1])
    send_grad[...] = back_input(weights[1], saved[1]).astype(BF16)
    grad_copies = down_halo(3, send_grad)
    for copy in grad_copies:
        copy.start()
    transpose_saved(saved[1])
    grads_mlp(saved[1], packs[1])
    grads_attention(saved[1], packs[1], total, beta_grad, spread_ref)
    whole.start()
    for copy in dec_copies:
        copy.wait()
    fold(unshifted(2, send_dec), fields[0])
    stores[0].start()
    transpose_saved(saved[0])
    beta_grad = back_mlp(send_grad[0:own, :].astype(F32), weights[0], saved[0], PIX - own)
    for copy in grad_copies:
        copy.wait()
    factor = 1.0 / math.sqrt(PIX * n_lat * n_lon)

    field[...] = unshifted(3, send_grad)
    beta_grad = beta_grad + back_mlp(field[0 : PIX - own, :], weights[0], saved[0], 0)
    grads_mlp(saved[0], packs[0])
    upper.start()
    total = back_attention(saved[0])
    grads_attention(saved[0], packs[0], total, beta_grad, spread_ref)
    lower.start()
    fold(back_input(weights[0], saved[0]), fields[1])
    stores[1].start()
    whole.add_plane()
    upper.add_plane()
    lower.add_plane()
    whole.add_all(factor)
    upper.add_all(factor)
    lower.add_all(factor)
    whole.finish()
    stores[3].start()
    upper.finish()
    lower.finish()
    stores[2].start()
    for store in stores:
        store.wait()


def solution(mesh):
    n_lat, n_lon = mesh.shape["lat"], mesh.shape["lon"]

    def per_device(sig, cot, wqkv, wproj, wup, wdown, gamma, beta, table):
        dma = pltpu.SemaphoreType.DMA
        args = (sig, cot, wqkv, wproj, wup, jnp.swapaxes(wdown, 1, 2), gamma, beta, jnp.swapaxes(table, 0, 1))
        saved = [pltpu.VMEM(shape, kind) for shape, kind in Saved.names.values()]
        scratch = [pltpu.VMEM(arg.shape, arg.dtype) for arg in args] + [dma((9,))]
        scratch += [pltpu.VMEM((RELS, SLOTS), BF16), pltpu.VMEM((HEADS * TOKENS, HEADS * 128), BF16)]
        scratch += saved + saved
        scratch += [pltpu.VMEM((PIX, C), F32)] + [pltpu.VMEM((PIX, C), BF16)] * 4
        scratch += [
            pltpu.VMEM((4, HALF, C), BF16),
            pltpu.VMEM((4, UNIT, C), BF16),
            pltpu.VMEM((4, UNIT, C), BF16),
            dma((12,)),
            dma((12,)),
        ]
        scratch += [pltpu.VMEM((ROWS, 128), BF16)] * 2 + [pltpu.VMEM(sig.shape, BF16)] * 2
        scratch += [pltpu.VMEM((ROWS, 128), BF16)] * 2 + [dma((4,))]
        scratch += exchange_scratch(n_lat, n_lon, ROWS)
        scratch += exchange_scratch(n_lat, n_lon, ROWS // 2) * 2
        hbm = pl.BlockSpec(memory_space=pltpu.HBM)
        field = jax.ShapeDtypeStruct(sig.shape, BF16)
        total = jax.ShapeDtypeStruct((ROWS, 128), BF16)
        results = pl.pallas_call(
            functools.partial(kernel, n_lat, n_lon),
            out_shape=[field, field, total, total],
            in_specs=[hbm] * 9,
            out_specs=[hbm] * 4,
            scratch_shapes=scratch,
            compiler_params=pltpu.CompilerParams(
                collective_id=0, has_side_effects=True, vmem_limit_bytes=62 * 1024 * 1024
            ),
        )(*args)
        grads = [jax.ShapeDtypeStruct(leaf.shape, F32) for leaf in args[2:]]
        outs = pl.pallas_call(
            unpack_kernel,
            out_shape=[field, field] + grads,
            in_specs=[hbm] * 4,
            out_specs=[hbm] * 9,
            scratch_shapes=[pltpu.VMEM(leaf.shape, F32) for leaf in args[2:]]
            + [pltpu.VMEM(sig.shape, BF16)] * 2
            + [pltpu.VMEM((ROWS, 128), BF16)] * 2
            + [dma((13,))],
            compiler_params=pltpu.CompilerParams(vmem_limit_bytes=62 * 1024 * 1024),
        )(*results)
        decoded, sgrad, qkv, proj, up, down, gammas, betas, tables = outs
        return decoded, sgrad, qkv, proj, up, jnp.swapaxes(down, 1, 2), gammas, betas, jnp.swapaxes(tables, 0, 1)

    in_specs = (P("lat", "lon"), P("lat", "lon"), P(), P(), P(), P(), P(), P(), P())
    out_specs = (P("lat", "lon"), P("lat", "lon"), P(), P(), P(), P(), P(), P(), P())
    return jax.shard_map(per_device, mesh=mesh, in_specs=in_specs, out_specs=out_specs, check_vma=False)
```

```python
import functools
import math

import jax
import jax.numpy as jnp
from jax import lax
from jax.experimental import pallas as pl
from jax.experimental.pallas import tpu as pltpu
from jax.sharding import PartitionSpec as P

C = 96
HEADS = 3
HEAD = 32
HID = 384
WIN = 8
RELS = 225
SLOTS = 256
PIX = 512
HALF = 256
UNIT = 16
WINDOWS = 8
TOKENS = 64
ROWS = 1024
QUAD = 4
EPS = 1e-05
GELU_A = math.sqrt(2.0 / math.pi)
GELU_B = 0.044715
MESH = pl.DeviceIdType.MESH
F32 = jnp.float32
BF16 = jnp.bfloat16


def iota(shape, dim):
    return lax.broadcasted_iota(jnp.int32, shape, dim)


def dot(a, b, over=(1, 0)):
    return lax.dot_general(a, b, (((over[0],), (over[1],)), ((), ())), preferred_element_type=F32)


def dot_split(a, b):
    high = a.astype(BF16)
    rest = a - high.astype(F32)
    middle = rest.astype(BF16)
    low = (rest - middle.astype(F32)).astype(BF16)
    return dot(high, b) + dot(middle, b) + dot(low, b)


def row_mean(a):
    return jnp.sum(a, axis=-1, keepdims=True) * (1.0 / C)


def normalise(v):
    center = v - row_mean(v)
    scale = lax.rsqrt(row_mean(center * center) + EPS)
    return center * scale, scale


def norm_back(grad, hat, scale):
    return scale * (grad - row_mean(grad) - hat * row_mean(grad * hat))


def stack_heads(a):
    head_of = iota(a.shape, 1) // HEAD
    zero = jnp.zeros_like(a)
    return jnp.concatenate([jnp.where(head_of == h, a, zero) for h in range(HEADS)], axis=0)


def merge_heads(a):
    parts = [a[h * TOKENS : (h + 1) * TOKENS] for h in range(HEADS)]
    head_of = iota((TOKENS, C), 1) // HEAD
    return jnp.where(head_of == 0, parts[0], jnp.where(head_of == 1, parts[1], parts[2]))


def window(ref, w):
    step = TOKENS // 2
    upper = ref[w * step : (w + 1) * step, :]
    lower = ref[HALF + w * step : HALF + (w + 1) * step, :]
    return jnp.concatenate([upper, lower], axis=0)


def put_window(ref, w, value):
    step = TOKENS // 2
    ref[w * step : (w + 1) * step, :] = value[:step].astype(ref.dtype)
    ref[HALF + w * step : HALF + (w + 1) * step, :] = value[step:].astype(ref.dtype)


def unfold(src, dst):
    low = iota((WIN, C), 0) < 4
    for group in range(16):
        part = src[:, group * 4 * C : (group + 1) * 4 * C].astype(F32)
        for pair in range(2):
            one = part[:, (2 * pair) * C : (2 * pair + 1) * C]
            two = part[:, (2 * pair + 1) * C : (2 * pair + 2) * C]
            at = (group * 2 + pair) * 8
            dst[at : at + 8, :] = jnp.where(low, one, pltpu.roll(two, 4, 0)).astype(dst.dtype)
            dst[HALF + at : HALF + at + 8, :] = jnp.where(low, pltpu.roll(one, 4, 0), two).astype(dst.dtype)


def fold(value, dst):
    low = iota((WIN, C), 0) < 4
    for group in range(16):
        parts = []
        for pair in range(2):
            at = (group * 2 + pair) * 8
            upper = value[at : at + 8]
            lower = value[HALF + at : HALF + at + 8]
            parts.append(jnp.where(low, upper, pltpu.roll(lower, 4, 0)))
            parts.append(jnp.where(low, pltpu.roll(upper, 4, 0), lower))
        dst[:, group * 4 * C : (group + 1) * 4 * C] = jnp.concatenate(parts, axis=1).astype(dst.dtype)


def rel_slots():
    entry = iota((RELS, SLOTS), 0)
    slot = iota((RELS, SLOTS), 1)
    return ((entry // 15 == slot % 16) & (entry % 15 == slot // 16)).astype(F32)


def spread_queries():
    query = iota((HEADS * TOKENS, HEADS * 128), 0)
    place = iota((HEADS * TOKENS, HEADS * 128), 1)
    inside = query % TOKENS
    row = (inside // 32) * 4 + inside % 4
    column = (inside % 32) // 4
    return ((query // TOKENS) * 128 + column * 16 + row == place).astype(F32)


def build_bias(table, slot_ref, spread_ref, bias):
    slots = dot_split(table, slot_ref[...])
    sub = iota((8, SLOTS), 0)
    heads = []
    for h in range(HEADS):
        line = jnp.broadcast_to(slots[h : h + 1], (8, SLOTS))
        skew = line
        for s in range(1, 8):
            skew = jnp.where(sub == s, pltpu.roll(line, 16 * (s // 4) + s % 4, 1), skew)
        groups = []
        for g in range(8):
            turn = SLOTS - 119 + 32 * (g % 4) + 4 * (g // 4)
            groups.append(pltpu.roll(skew, turn % SLOTS, 1)[:, :128])
        heads.append(jnp.concatenate(groups, axis=0))
    wide = jnp.concatenate(heads, axis=1)
    back = spread_ref[...]
    high = wide.astype(BF16)
    rest = wide - high.astype(F32)
    middle = rest.astype(BF16)
    low = (rest - middle.astype(F32)).astype(BF16)
    bias[...] = dot(high, back, (1, 1)) + dot(middle, back, (1, 1)) + dot(low, back, (1, 1))


def table_slots(total, spread_ref):
    wide = dot(total.astype(BF16), spread_ref[...])
    sub = iota((8, SLOTS), 0)
    blank = jnp.zeros((8, 128), F32)
    lines = []
    for h in range(HEADS):
        skew = jnp.zeros((8, SLOTS), F32)
        for g in range(8):
            part = jnp.concatenate([wide[8 * g : 8 * g + 8, 128 * h : 128 * h + 128], blank], axis=1)
            skew = skew + pltpu.roll(part, 119 - 32 * (g % 4) - 4 * (g // 4), 1)
        line = skew
        for s in range(1, 8):
            line = jnp.where(sub == s, pltpu.roll(skew, SLOTS - 16 * (s // 4) - s % 4, 1), line)
        lines.append(jnp.sum(line, axis=0, keepdims=True))
    return lines


def gelu_parts(up):
    square = up * up
    bent = jnp.tanh(GELU_A * up * (1.0 + GELU_B * square))
    return square, bent, 0.5 * (1.0 + bent)


def gelu_slope(up, square, bent, half):
    return half + 0.5 * up * (1.0 - bent * bent) * (GELU_A * (1.0 + 3.0 * GELU_B * square))


def project(x, weights, saved, start):
    rows = slice(start, start + x.shape[0])
    wq, wk, wv = weights[0]
    hat, scale = normalise(x)
    saved.hat1[rows, :] = hat
    saved.scale1[rows, :] = scale
    normed = hat.astype(BF16)
    saved.query[rows, :] = dot(normed, wq).astype(BF16)
    saved.key[rows, :] = dot(normed, wk).astype(BF16)
    saved.value[rows, :] = dot(normed, wv).astype(BF16)


def forward(x, weights, saved, blocked, slope_later):
    _, wproj, wup, wdown, gamma, beta = weights
    bias = saved.bias[...]
    every = range(WINDOWS)
    scores = [dot(window(saved.key, w), stack_heads(window(saved.query, w)), (1, 1)) for w in every]
    scores = [score * (HEAD**-0.5) + bias for score in scores]
    if blocked is not None:
        scores = [jnp.where(blocked, -1e9, score) for score in scores]
    scores = [jnp.exp(score - jnp.max(score, axis=0, keepdims=True)) for score in scores]
    attns = [score / jnp.sum(score, axis=0, keepdims=True) for score in scores]
    for w in every:
        saved.attn[w] = attns[w]
    mixed = [dot(attns[w].astype(BF16), window(saved.value, w), (0, 0)) for w in every]
    for w in every:
        put_window(saved.mixed, w, merge_heads(mixed[w]))
    hidden = x + dot(saved.mixed[...], wproj)
    hat, scale = normalise(hidden)
    saved.hat2[...] = hat
    saved.scale2[...] = scale
    up = dot(hat.astype(BF16), wup)
    square, bent, half = gelu_parts(up)
    lifted = (up * half).astype(BF16)
    saved.lifted[...] = lifted
    saved.slope[...] = up if slope_later else gelu_slope(up, square, bent, half)
    gdn = hidden + dot(lifted, wdown, (1, 1))
    power = beta + dot((gdn * gdn).astype(BF16), gamma)
    root = lax.rsqrt(power)
    saved.gdn[...] = gdn
    saved.root[...] = root
    return gdn * root


def prepare(saved):
    up = saved.slope[...]
    saved.slope[...] = gelu_slope(up, *gelu_parts(up))


def transpose_saved(saved):
    saved.normed_t[...] = saved.hat1[...].T.astype(BF16)
    saved.hat2_t[...] = saved.hat2[...].T.astype(BF16)
    saved.mixed_t[...] = saved.mixed[...].astype(F32).T.astype(BF16)
    gdn = saved.gdn[...]
    saved.square_t[...] = (gdn * gdn).T.astype(BF16)


def back_mlp(grad, weights, saved, start):
    rows = slice(start, start + grad.shape[0])
    _, wproj, wup, wdown, gamma, _ = weights
    gdn = saved.gdn[rows, :]
    root = saved.root[rows, :]
    dpower = -0.5 * grad * gdn * (root * root * root)
    dpower_16 = dpower.astype(BF16)
    saved.dpower[rows, :] = dpower_16
    dgdn = grad * root + 2.0 * gdn * dot(dpower_16, gamma, (1, 1))
    dgdn_16 = dgdn.astype(BF16)
    saved.dgdn[rows, :] = dgdn_16
    dup = (dot(dgdn_16, wdown) * saved.slope[rows, :]).astype(BF16)
    saved.dup[rows, :] = dup
    dhidden = dgdn + norm_back(dot(dup, wup, (1, 1)), saved.hat2[rows, :], saved.scale2[rows, :])
    dhidden_16 = dhidden.astype(BF16)
    saved.dhidden[rows, :] = dhidden_16
    saved.dmixed[rows, :] = dot(dhidden_16, wproj, (1, 1)).astype(BF16)
    saved.wide[rows, :] = dhidden
    return jnp.sum(dpower, axis=0, keepdims=True)


def grads_mlp(saved, pack):
    down_grad = dot(saved.dgdn[...], saved.lifted[...], (0, 0))
    up_grad = dot(saved.hat2_t[...], saved.dup[...])
    gamma_grad = dot(saved.square_t[...], saved.dpower[...])
    for i in range(3):
        pack[C * i : C * (i + 1), :] = up_grad[:, 128 * i : 128 * (i + 1)].astype(BF16)
        pack[288 + C * i : 288 + C * (i + 1), :] = down_grad[:, 128 * i : 128 * (i + 1)].astype(BF16)
        pack[576 + C * i : 576 + C * (i + 1), C:128] = gamma_grad[:, 32 * i : 32 * (i + 1)].astype(BF16)
    pack[864:960, 0:C] = dot(saved.mixed_t[...], saved.dhidden[...]).astype(BF16)


def back_attention(saved):
    every = range(WINDOWS)
    dmixed = [stack_heads(window(saved.dmixed, w)) for w in every]
    dattns = [dot(window(saved.value, w), dmixed[w], (1, 1)) for w in every]
    dvalues = [dot(saved.attn[w].astype(BF16), dmixed[w]) for w in every]
    for w in every:
        put_window(saved.dvalue, w, dvalues[w])
    dscores = []
    for w in every:
        attn = saved.attn[w]
        dscores.append(attn * (dattns[w] - jnp.sum(attn * dattns[w], axis=0, keepdims=True)))
    total = dscores[0]
    for w in every[1:]:
        total = total + dscores[w]
    dscores = [(dscore * (HEAD**-0.5)).astype(BF16) for dscore in dscores]
    dqueries = [dot(dscores[w], window(saved.key, w), (0, 0)) for w in every]
    dkeys = [dot(dscores[w], stack_heads(window(saved.query, w))) for w in every]
    for w in every:
        put_window(saved.dkey, w, dkeys[w])
        put_window(saved.dquery, w, merge_heads(dqueries[w]))
    return total


def grads_attention(saved, pack, total, beta_grad, spread_ref):
    for i, part in enumerate((saved.dquery, saved.dkey, saved.dvalue)):
        pack[576 + C * i : 576 + C * (i + 1), 0:C] = dot(saved.normed_t[...], part[...]).astype(BF16)
    edge = jnp.concatenate([beta_grad, jnp.zeros((1, 128 - C), F32)], axis=1)
    lines = table_slots(total, spread_ref)
    rows = [edge] + [line[:, 128 * i : 128 * (i + 1)] for line in lines for i in range(2)]
    rows.append(jnp.zeros((ROWS - 967, 128), F32))
    pack[960:ROWS, :] = jnp.concatenate(rows, axis=0).astype(BF16)


def back_input(weights, saved):
    wq, wk, wv = weights[0]
    dnormed = dot(saved.dquery[...], wq, (1, 1)) + dot(saved.dkey[...], wk, (1, 1)) + dot(saved.dvalue[...], wv, (1, 1))
    return saved.wide[...] + norm_back(dnormed, saved.hat1[...], saved.scale1[...])


class Saved:
    names = {
        "hat1": ((PIX, C), F32),
        "scale1": ((PIX, 1), F32),
        "query": ((PIX, C), BF16),
        "key": ((PIX, C), BF16),
        "value": ((PIX, C), BF16),
        "bias": ((TOKENS, HEADS * TOKENS), F32),
        "attn": ((WINDOWS, TOKENS, HEADS * TOKENS), F32),
        "mixed": ((PIX, C), BF16),
        "hat2": ((PIX, C), F32),
        "scale2": ((PIX, 1), F32),
        "lifted": ((PIX, HID), BF16),
        "slope": ((PIX, HID), F32),
        "gdn": ((PIX, C), F32),
        "root": ((PIX, C), F32),
        "dmixed": ((PIX, C), BF16),
        "dquery": ((PIX, C), BF16),
        "dkey": ((PIX, C), BF16),
        "dvalue": ((PIX, C), BF16),
        "dpower": ((PIX, C), BF16),
        "dgdn": ((PIX, C), BF16),
        "dup": ((PIX, HID), BF16),
        "dhidden": ((PIX, C), BF16),
        "wide": ((PIX, C), F32),
        "normed_t": ((C, PIX), BF16),
        "hat2_t": ((C, PIX), BF16),
        "mixed_t": ((C, PIX), BF16),
        "square_t": ((C, PIX), BF16),
    }

    def __init__(self, refs):
        for name, ref in zip(Saved.names, refs):
            setattr(self, name, ref)


def copy_to(src, dst, send, recv, device):
    return pltpu.make_async_remote_copy(
        src_ref=src, dst_ref=dst, send_sem=send, recv_sem=recv, device_id=device, device_id_type=MESH
    )


def read_weights(b, refs):
    wqkv, wproj, wup, wdown, gamma, beta = refs
    whole = wqkv[b].astype(F32)
    parts = tuple(whole[:, C * i : C * (i + 1)].astype(BF16) for i in range(3))
    return parts, wproj[b], wup[b], wdown[b], gamma[b].astype(BF16), beta[b : b + 1, :]


class Exchange:
    width = QUAD
    turns = (2, 1, 3, 0)

    def __init__(self, n_lat, n_lon, base, pack, total, first, planes, mine, sems):
        self.n_lat, self.planes_n, self.size = n_lat, n_lon // QUAD, n_lat * self.width
        self.lat, self.lon = lax.axis_index("lat"), lax.axis_index("lon")
        self.z = self.lon // QUAD
        self.quad = self.column(self.lon)
        self.base, self.pack, self.total = base, pack, total
        self.first, self.planes, self.mine, self.sems = first, planes, mine, sems
        self.rows = first.shape[1]
        self.place = self.lat * self.width + self.quad

    def column(self, lon):
        return lax.rem(lon, QUAD)

    def device_of(self, lat, quad):
        return (lat, self.z * QUAD + quad)

    def piece(self, ref, i):
        return ref.at[pl.ds(pl.multiple_of(self.base + i * self.rows, UNIT), self.rows), :]

    def in_plane(self, make):
        def body(i, _):
            step = lax.rem(4 * i + 1, 7) + 1 if self.n_lat == 8 else i + 1
            for turn in self.turns:
                make(step, turn).start()
            return 0

        lax.fori_loop(0, self.n_lat - 1, body, 0)
        for turn in self.turns[:-1]:
            make(0, turn).start()

    def target(self, step, turn):
        lat = lax.rem(self.lat + step, self.n_lat)
        quad = lax.rem(self.quad + turn, self.width)
        return lat * self.width + quad, self.device_of(lat, quad)

    def scatter_copy(self, step, turn):
        place, device = self.target(step, turn)
        slot = self.first.at[step * self.width + turn]
        return copy_to(self.piece(self.pack, place), slot, self.sems.at[0], self.sems.at[1], device)

    def gather_copy(self, step, turn):
        _, device = self.target(step, turn)
        return copy_to(self.mine, self.piece(self.total, self.place), self.sems.at[4], self.sems.at[5], device)

    def own_copy(self):
        return pltpu.make_async_copy(self.mine, self.piece(self.total, self.place), self.sems.at[6])

    def plane_copy(self, step):
        slot = self.planes.at[self.z]
        device = (self.lat, lax.rem(self.lon + step * QUAD, self.planes_n * QUAD))
        return copy_to(slot, slot, self.sems.at[2], self.sems.at[3], device)

    def wait_both(self, ref, sem):
        for i in range(2):
            pltpu.make_async_copy(ref, ref, self.sems.at[sem + i]).wait()

    def start(self):
        self.in_plane(self.scatter_copy)

    def add_plane(self):
        self.wait_both(self.first.at[pl.ds(1, self.size - 1)], 0)
        total = self.piece(self.pack, self.place)[...].astype(F32)
        for i in range(1, self.size):
            total = total + self.first[i].astype(F32)
        self.planes[self.z] = total.astype(BF16)

        def body(step, _):
            self.plane_copy(step).start()
            return 0

        lax.fori_loop(1, self.planes_n, body, 0)

    def add_all(self, factor):
        if self.planes_n > 1:
            self.wait_both(self.planes.at[pl.ds(0, self.planes_n - 1)], 2)
        total = self.planes[0].astype(F32)
        for i in range(1, self.planes_n):
            total = total + self.planes[i].astype(F32)
        self.mine[...] = (total * factor).astype(BF16)
        self.in_plane(self.gather_copy)
        self.own_copy().start()

    def finish(self):
        self.wait_both(self.total.at[pl.ds(0, (self.size - 1) * self.rows), :], 4)
        self.own_copy().wait()


class PairedExchange(Exchange):
    width = QUAD // 2
    turns = (1, 0)

    def __init__(self, n_lat, n_lon, pack, total, half, first, planes, mine, sems):
        self.half = half
        self.core = lax.rem(lax.axis_index("lon"), 2)
        super().__init__(n_lat, n_lon, self.core * (ROWS // 2), pack, total, first, planes, mine, sems)

    def column(self, lon):
        return lax.rem(lon, QUAD) // 2

    def device_of(self, lat, quad):
        return (lat, self.z * QUAD + quad * 2 + self.core)

    def half_of(self, ref, core):
        return ref.at[pl.ds(pl.multiple_of(core * (ROWS // 2), ROWS // 2), ROWS // 2), :]

    def pair_copy(self):
        device = (self.lat, self.lon + 1 - 2 * self.core)
        return copy_to(self.half_of(self.pack, 1 - self.core), self.half, self.sems.at[7], self.sems.at[8], device)

    def swap_copy(self):
        device = (self.lat, self.lon + 1 - 2 * self.core)
        mine = self.half_of(self.total, self.core)
        return copy_to(mine, mine, self.sems.at[9], self.sems.at[10], device)

    def start_pair(self):
        self.pair_copy().start()

    def add_pair(self):
        self.pair_copy().wait()
        mine = self.half_of(self.pack, self.core)
        mine[...] = (mine[...].astype(F32) + self.half[...].astype(F32)).astype(BF16)
        self.start()

    def swap(self):
        super().finish()
        self.swap_copy().start()

    def finish(self):
        self.swap_copy().wait()


def exchange_scratch(n_lat, n_lon, rows, members):
    rows = rows // members
    return [
        pltpu.VMEM((members, rows, 128), BF16),
        pltpu.VMEM((n_lon // QUAD, rows, 128), BF16),
        pltpu.VMEM((rows, 128), BF16),
        pltpu.SemaphoreType.DMA((11,)),
    ]


def unpack(b, total, outs):
    qkv, proj, up, down, gamma, beta, table = outs
    first = total[576:864, :].astype(F32)
    parts = [first[C * i : C * (i + 1)] for i in range(3)]
    qkv[b] = jnp.concatenate([part[:, 0:C] for part in parts], axis=1)
    gamma[b] = jnp.concatenate([part[:, C:128] for part in parts], axis=1)
    proj[b] = total[864:960, 0:C].astype(F32)
    for i in range(3):
        up[b, :, 128 * i : 128 * (i + 1)] = total[C * i : C * (i + 1), :].astype(F32)
        down[b, :, 128 * i : 128 * (i + 1)] = total[288 + C * i : 288 + C * (i + 1), :].astype(F32)
    edge = total[960:976, :].astype(F32)
    beta[b : b + 1, :] = edge[0:1, 0:C]
    lines = [jnp.concatenate([edge[1 + 2 * h : 2 + 2 * h], edge[2 + 2 * h : 3 + 2 * h]], axis=1) for h in range(HEADS)]
    slots = jnp.concatenate(lines, axis=0).astype(BF16)
    table[:, b, :] = dot(slots, rel_slots().astype(BF16), (1, 1))


def unpack_kernel(*refs):
    ins, outs, staged, held, sems = refs[:4], refs[4:13], refs[13:20], refs[20:24], refs[24]
    loads = [pltpu.make_async_copy(src, dst, sems.at[9 + i]) for i, (src, dst) in enumerate(zip(ins, held))]
    sources = tuple(held[:2]) + tuple(staged)
    copies = [pltpu.make_async_copy(src, dst, sems.at[i]) for i, (src, dst) in enumerate(zip(sources, outs))]
    for i in (2, 3, 0, 1):
        loads[i].start()
    for b in range(2):
        loads[2 + b].wait()
        unpack(b, held[2 + b], staged)
    for i in range(2):
        loads[i].wait()
    for copy in copies:
        copy.start()
    for copy in copies:
        copy.wait()


def kernel(n_lat, n_lon, *refs):
    refs = list(refs)

    def take(count):
        taken = refs[:count]
        del refs[:count]
        return taken

    hbm_args = take(9)
    results = take(4)
    args = take(9)
    arg_sems, slot_ref, spread_ref = take(3)
    saved = [Saved(take(len(Saved.names))) for _ in range(2)]
    field, send_out, send_cot, send_dec, send_grad = take(5)
    south, east, corner, halo_send, halo_recv = take(5)
    packs, fields = take(2), take(2)
    (staged,) = take(1)
    (result_sems,) = take(1)
    whole = PairedExchange(n_lat, n_lon, packs[1], staged, *take(5))
    upper = Exchange(n_lat, n_lon, 0, packs[0], results[2], *take(4))
    lower = Exchange(n_lat, n_lon, ROWS // 2, packs[0], results[2], *take(4))
    lat, lon = lax.axis_index("lat"), lax.axis_index("lon")
    above, below = lax.rem(lat + n_lat - 1, n_lat), lax.rem(lat + 1, n_lat)
    west, easterly = lax.rem(lon + n_lon - 1, n_lon), lax.rem(lon + 1, n_lon)

    stores = [
        pltpu.make_async_copy(src, dst, result_sems.at[i]) for i, (src, dst) in enumerate(zip(fields + [staged], results[:2] + results[3:]))
    ]
    loads = [pltpu.make_async_copy(src, dst, arg_sems.at[i]) for i, (src, dst) in enumerate(zip(hbm_args, args))]
    for load in loads:
        load.start()
    barrier = pltpu.get_barrier_semaphore()

    def greet(device):
        pl.semaphore_signal(barrier, inc=1, device_id=device, device_id_type=MESH)

    def greet_plane(i, _):
        _, device = upper.target(i // QUAD, lax.rem(i, QUAD))
        greet(device)
        return 0

    def greet_planes(i, _):
        greet((lat, lax.rem(lon + QUAD * i, n_lon)))
        return 0

    planes_n = n_lon // QUAD
    lax.fori_loop(1, n_lat * QUAD, greet_plane, 0)
    lax.fori_loop(1, planes_n, greet_planes, 0)
    for device in ((lat, west), (lat, easterly), (above, west), (below, easterly)):
        greet(device)
    greetings = n_lat * QUAD + planes_n + 2

    def halo(i, ref, rows, devices):
        copies = []
        for j, target in enumerate((south, east, corner)):
            src = ref.at[pl.ds(rows[j][0], rows[j][1]), :]
            k = 3 * i + j
            copies.append(copy_to(src, target.at[i], halo_send.at[k], halo_recv.at[k], devices[j]))
        return copies

    def up_halo(i, ref):
        rows = ((0, HALF), (HALF, UNIT), (0, UNIT))
        return halo(i, ref, rows, ((above, lon), (lat, west), (above, west)))

    def down_halo(i, ref):
        rows = ((HALF, HALF), (HALF - UNIT, UNIT), (PIX - UNIT, UNIT))
        return halo(i, ref, rows, ((below, lon), (lat, easterly), (below, easterly)))

    def shifted(i, ref):
        parts = [ref[HALF + UNIT : PIX, :], east[i], south[i, UNIT:HALF, :], corner[i]]
        return jnp.concatenate([part.astype(F32) for part in parts], axis=0)

    def unshifted(i, ref):
        parts = [corner[i], south[i, 0 : HALF - UNIT, :], east[i], ref[0 : HALF - UNIT, :]]
        return jnp.concatenate([part.astype(F32) for part in parts], axis=0)

    sig, cot, table = args[0], args[1], args[8]
    slot_ref[...] = rel_slots().astype(BF16)
    spread_ref[...] = spread_queries().astype(BF16)
    loads[8].wait()
    build_bias(table[:, 0, :], slot_ref, spread_ref, saved[0].bias)
    for load in loads[:8]:
        load.wait()
    unfold(sig, field)
    weights = [read_weights(0, args[2:8])]
    project(field[...], weights[0], saved[0], 0)
    output = forward(field[...], weights[0], saved[0], None, True)
    send_out[...] = output.astype(BF16)

    pl.semaphore_wait(barrier, greetings)
    out_copies = up_halo(0, send_out)
    for copy in out_copies:
        copy.start()
    unfold(cot, send_cot)
    cot_copies = up_halo(1, send_cot)
    for copy in cot_copies:
        copy.start()
    build_bias(table[:, 1, :], slot_ref, spread_ref, saved[1].bias)
    is_last = (lat == n_lat - 1).astype(jnp.int32)
    shape = (TOKENS, HEADS * TOKENS)
    differ = (iota(shape, 0) // 32 != (iota(shape, 1) % TOKENS) // 32).astype(jnp.int32)
    blocked = differ * is_last > 0
    weights.append(read_weights(1, args[2:8]))
    own = HALF - UNIT
    project(send_out[HALF + UNIT : PIX, :].astype(F32), weights[1], saved[1], 0)
    prepare(saved[0])
    for copy in out_copies:
        copy.wait()
    field[...] = shifted(0, send_out)
    project(field[own:PIX, :], weights[1], saved[1], own)
    output = forward(field[...], weights[1], saved[1], blocked, False)
    send_dec[...] = output.astype(BF16)
    dec_copies = down_halo(2, send_dec)
    for copy in dec_copies:
        copy.start()
    for copy in cot_copies:
        copy.wait()
    beta_grad = back_mlp(shifted(1, send_cot), weights[1], saved[1], 0)
    total = back_attention(saved[1])
    send_grad[...] = back_input(weights[1], saved[1]).astype(BF16)
    grad_copies = down_halo(3, send_grad)
    for copy in grad_copies:
        copy.start()
    transpose_saved(saved[1])
    grads_mlp(saved[1], packs[1])
    grads_attention(saved[1], packs[1], total, beta_grad, spread_ref)
    whole.start_pair()
    for copy in dec_copies:
        copy.wait()
    fold(unshifted(2, send_dec), fields[0])
    stores[0].start()
    transpose_saved(saved[0])
    beta_grad = back_mlp(send_grad[0:own, :].astype(F32), weights[0], saved[0], PIX - own)
    whole.add_pair()
    for copy in grad_copies:
        copy.wait()
    factor = 1.0 / math.sqrt(PIX * n_lat * n_lon)

    field[...] = unshifted(3, send_grad)
    beta_grad = beta_grad + back_mlp(field[0 : PIX - own, :], weights[0], saved[0], 0)
    grads_mlp(saved[0], packs[0])
    upper.start()
    total = back_attention(saved[0])
    grads_attention(saved[0], packs[0], total, beta_grad, spread_ref)
    lower.start()
    fold(back_input(weights[0], saved[0]), fields[1])
    stores[1].start()
    whole.add_plane()
    upper.add_plane()
    lower.add_plane()
    whole.add_all(factor)
    upper.add_all(factor)
    lower.add_all(factor)
    whole.swap()
    upper.finish()
    whole.finish()
    stores[2].start()
    lower.finish()
    for store in stores:
        store.wait()


def solution(mesh):
    n_lat, n_lon = mesh.shape["lat"], mesh.shape["lon"]

    def per_device(sig, cot, wqkv, wproj, wup, wdown, gamma, beta, table):
        dma = pltpu.SemaphoreType.DMA
        args = (sig, cot, wqkv, wproj, wup, jnp.swapaxes(wdown, 1, 2), gamma, beta, jnp.swapaxes(table, 0, 1))
        saved = [pltpu.VMEM(shape, kind) for shape, kind in Saved.names.values()]
        scratch = [pltpu.VMEM(arg.shape, arg.dtype) for arg in args] + [dma((9,))]
        scratch += [pltpu.VMEM((RELS, SLOTS), BF16), pltpu.VMEM((HEADS * TOKENS, HEADS * 128), BF16)]
        scratch += saved + saved
        scratch += [pltpu.VMEM((PIX, C), F32)] + [pltpu.VMEM((PIX, C), BF16)] * 4
        scratch += [
            pltpu.VMEM((4, HALF, C), BF16),
            pltpu.VMEM((4, UNIT, C), BF16),
            pltpu.VMEM((4, UNIT, C), BF16),
            dma((12,)),
            dma((12,)),
        ]
        scratch += [pltpu.VMEM((ROWS, 128), BF16)] * 2 + [pltpu.VMEM(sig.shape, BF16)] * 2
        scratch += [pltpu.VMEM((ROWS, 128), BF16), dma((3,))]
        scratch += [pltpu.VMEM((ROWS // 2, 128), BF16)]
        scratch += exchange_scratch(n_lat, n_lon, ROWS // 2, n_lat * QUAD // 2)
        scratch += exchange_scratch(n_lat, n_lon, ROWS // 2, n_lat * QUAD) * 2
        hbm = pl.BlockSpec(memory_space=pltpu.HBM)
        field = jax.ShapeDtypeStruct(sig.shape, BF16)
        total = jax.ShapeDtypeStruct((ROWS, 128), BF16)
        results = pl.pallas_call(
            functools.partial(kernel, n_lat, n_lon),
            out_shape=[field, field, total, total],
            in_specs=[hbm] * 9,
            out_specs=[hbm] * 4,
            scratch_shapes=scratch,
            compiler_params=pltpu.CompilerParams(
                collective_id=0, has_side_effects=True, vmem_limit_bytes=62 * 1024 * 1024
            ),
        )(*args)
        grads = [jax.ShapeDtypeStruct(leaf.shape, F32) for leaf in args[2:]]
        outs = pl.pallas_call(
            unpack_kernel,
            out_shape=[field, field] + grads,
            in_specs=[hbm] * 4,
            out_specs=[hbm] * 9,
            scratch_shapes=[pltpu.VMEM(leaf.shape, F32) for leaf in args[2:]]
            + [pltpu.VMEM(sig.shape, BF16)] * 2
            + [pltpu.VMEM((ROWS, 128), BF16)] * 2
            + [dma((13,))],
            compiler_params=pltpu.CompilerParams(vmem_limit_bytes=62 * 1024 * 1024),
        )(*results)
        decoded, sgrad, qkv, proj, up, down, gammas, betas, tables = outs
        return decoded, sgrad, qkv, proj, up, jnp.swapaxes(down, 1, 2), gammas, betas, jnp.swapaxes(tables, 0, 1)

    in_specs = (P("lat", "lon"), P("lat", "lon"), P(), P(), P(), P(), P(), P(), P())
    out_specs = (P("lat", "lon"), P("lat", "lon"), P(), P(), P(), P(), P(), P(), P())
    return jax.shard_map(per_device, mesh=mesh, in_specs=in_specs, out_specs=out_specs, check_vma=False)
```

```python
import functools
import math

import jax
import jax.numpy as jnp
from jax import lax
from jax.experimental import pallas as pl
from jax.experimental.pallas import tpu as pltpu
from jax.sharding import PartitionSpec as P

C = 96
HEADS = 3
HEAD = 32
HID = 384
WIN = 8
RELS = 225
SLOTS = 256
PIX = 512
HALF = 256
UNIT = 16
WINDOWS = 8
TOKENS = 64
ROWS = 1024
QUAD = 4
EPS = 1e-05
GELU_A = math.sqrt(2.0 / math.pi)
GELU_B = 0.044715
MESH = pl.DeviceIdType.MESH
F32 = jnp.float32
BF16 = jnp.bfloat16


def iota(shape, dim):
    return lax.broadcasted_iota(jnp.int32, shape, dim)


def dot(a, b, over=(1, 0)):
    return lax.dot_general(a, b, (((over[0],), (over[1],)), ((), ())), preferred_element_type=F32)


def dot_split(a, b):
    high = a.astype(BF16)
    rest = a - high.astype(F32)
    middle = rest.astype(BF16)
    low = (rest - middle.astype(F32)).astype(BF16)
    return dot(high, b) + dot(middle, b) + dot(low, b)


def row_mean(a):
    return jnp.sum(a, axis=-1, keepdims=True) * (1.0 / C)


def normalise(v):
    center = v - row_mean(v)
    scale = lax.rsqrt(row_mean(center * center) + EPS)
    return center * scale, scale


def norm_back(grad, hat, scale):
    return scale * (grad - row_mean(grad) - hat * row_mean(grad * hat))


def stack_heads(a):
    head_of = iota(a.shape, 1) // HEAD
    zero = jnp.zeros_like(a)
    return jnp.concatenate([jnp.where(head_of == h, a, zero) for h in range(HEADS)], axis=0)


def merge_heads(a):
    parts = [a[h * TOKENS : (h + 1) * TOKENS] for h in range(HEADS)]
    head_of = iota((TOKENS, C), 1) // HEAD
    return jnp.where(head_of == 0, parts[0], jnp.where(head_of == 1, parts[1], parts[2]))


def window(ref, w):
    step = TOKENS // 2
    upper = ref[w * step : (w + 1) * step, :]
    lower = ref[HALF + w * step : HALF + (w + 1) * step, :]
    return jnp.concatenate([upper, lower], axis=0)


def put_window(ref, w, value):
    step = TOKENS // 2
    ref[w * step : (w + 1) * step, :] = value[:step].astype(ref.dtype)
    ref[HALF + w * step : HALF + (w + 1) * step, :] = value[step:].astype(ref.dtype)


def unfold(src, dst):
    low = iota((WIN, C), 0) < 4
    for group in range(16):
        part = src[:, group * 4 * C : (group + 1) * 4 * C].astype(F32)
        for pair in range(2):
            one = part[:, (2 * pair) * C : (2 * pair + 1) * C]
            two = part[:, (2 * pair + 1) * C : (2 * pair + 2) * C]
            at = (group * 2 + pair) * 8
            dst[at : at + 8, :] = jnp.where(low, one, pltpu.roll(two, 4, 0)).astype(dst.dtype)
            dst[HALF + at : HALF + at + 8, :] = jnp.where(low, pltpu.roll(one, 4, 0), two).astype(dst.dtype)


def fold(value, dst):
    low = iota((WIN, C), 0) < 4
    for group in range(16):
        parts = []
        for pair in range(2):
            at = (group * 2 + pair) * 8
            upper = value[at : at + 8]
            lower = value[HALF + at : HALF + at + 8]
            parts.append(jnp.where(low, upper, pltpu.roll(lower, 4, 0)))
            parts.append(jnp.where(low, pltpu.roll(upper, 4, 0), lower))
        dst[:, group * 4 * C : (group + 1) * 4 * C] = jnp.concatenate(parts, axis=1).astype(dst.dtype)


def rel_slots():
    entry = iota((RELS, SLOTS), 0)
    slot = iota((RELS, SLOTS), 1)
    return ((entry // 15 == slot % 16) & (entry % 15 == slot // 16)).astype(F32)


def spread_queries():
    query = iota((HEADS * TOKENS, HEADS * 128), 0)
    place = iota((HEADS * TOKENS, HEADS * 128), 1)
    inside = query % TOKENS
    row = (inside // 32) * 4 + inside % 4
    column = (inside % 32) // 4
    return ((query // TOKENS) * 128 + column * 16 + row == place).astype(F32)


def build_bias(table, slot_ref, spread_ref, bias):
    slots = dot_split(table, slot_ref[...])
    sub = iota((8, SLOTS), 0)
    heads = []
    for h in range(HEADS):
        line = jnp.broadcast_to(slots[h : h + 1], (8, SLOTS))
        skew = line
        for s in range(1, 8):
            skew = jnp.where(sub == s, pltpu.roll(line, 16 * (s // 4) + s % 4, 1), skew)
        groups = []
        for g in range(8):
            turn = SLOTS - 119 + 32 * (g % 4) + 4 * (g // 4)
            groups.append(pltpu.roll(skew, turn % SLOTS, 1)[:, :128])
        heads.append(jnp.concatenate(groups, axis=0))
    wide = jnp.concatenate(heads, axis=1)
    back = spread_ref[...]
    high = wide.astype(BF16)
    rest = wide - high.astype(F32)
    middle = rest.astype(BF16)
    low = (rest - middle.astype(F32)).astype(BF16)
    bias[...] = dot(high, back, (1, 1)) + dot(middle, back, (1, 1)) + dot(low, back, (1, 1))


def table_slots(total, spread_ref):
    wide = dot(total.astype(BF16), spread_ref[...])
    sub = iota((8, SLOTS), 0)
    blank = jnp.zeros((8, 128), F32)
    lines = []
    for h in range(HEADS):
        skew = jnp.zeros((8, SLOTS), F32)
        for g in range(8):
            part = jnp.concatenate([wide[8 * g : 8 * g + 8, 128 * h : 128 * h + 128], blank], axis=1)
            skew = skew + pltpu.roll(part, 119 - 32 * (g % 4) - 4 * (g // 4), 1)
        line = skew
        for s in range(1, 8):
            line = jnp.where(sub == s, pltpu.roll(skew, SLOTS - 16 * (s // 4) - s % 4, 1), line)
        lines.append(jnp.sum(line, axis=0, keepdims=True))
    return lines


def gelu_parts(up):
    square = up * up
    bent = jnp.tanh(GELU_A * up * (1.0 + GELU_B * square))
    return square, bent, 0.5 * (1.0 + bent)


def gelu_slope(up, square, bent, half):
    return half + 0.5 * up * (1.0 - bent * bent) * (GELU_A * (1.0 + 3.0 * GELU_B * square))


def project(x, weights, saved, start):
    rows = slice(start, start + x.shape[0])
    wq, wk, wv = weights[0]
    hat, scale = normalise(x)
    saved.hat1[rows, :] = hat
    saved.scale1[rows, :] = scale
    normed = hat.astype(BF16)
    saved.query[rows, :] = dot(normed, wq).astype(BF16)
    saved.key[rows, :] = dot(normed, wk).astype(BF16)
    saved.value[rows, :] = dot(normed, wv).astype(BF16)


def forward(x, weights, saved, blocked, slope_later):
    _, wproj, wup, wdown, gamma, beta = weights
    bias = saved.bias[...]
    every = range(WINDOWS)
    scores = [dot(window(saved.key, w), stack_heads(window(saved.query, w)), (1, 1)) for w in every]
    scores = [score * (HEAD**-0.5) + bias for score in scores]
    if blocked is not None:
        scores = [jnp.where(blocked, -1e9, score) for score in scores]
    scores = [jnp.exp(score - jnp.max(score, axis=0, keepdims=True)) for score in scores]
    attns = [score / jnp.sum(score, axis=0, keepdims=True) for score in scores]
    for w in every:
        saved.attn[w] = attns[w]
    mixed = [dot(attns[w].astype(BF16), window(saved.value, w), (0, 0)) for w in every]
    for w in every:
        put_window(saved.mixed, w, merge_heads(mixed[w]))
    hidden = x + dot(saved.mixed[...], wproj)
    hat, scale = normalise(hidden)
    saved.hat2[...] = hat
    saved.scale2[...] = scale
    up = dot(hat.astype(BF16), wup)
    square, bent, half = gelu_parts(up)
    lifted = (up * half).astype(BF16)
    saved.lifted[...] = lifted
    saved.slope[...] = up if slope_later else gelu_slope(up, square, bent, half)
    gdn = hidden + dot(lifted, wdown, (1, 1))
    power = beta + dot((gdn * gdn).astype(BF16), gamma)
    root = lax.rsqrt(power)
    saved.gdn[...] = gdn
    saved.root[...] = root
    return gdn * root


def prepare(saved):
    up = saved.slope[...]
    saved.slope[...] = gelu_slope(up, *gelu_parts(up))


def transpose_saved(saved):
    saved.normed_t[...] = saved.hat1[...].T.astype(BF16)
    saved.hat2_t[...] = saved.hat2[...].T.astype(BF16)
    saved.mixed_t[...] = saved.mixed[...].astype(F32).T.astype(BF16)
    gdn = saved.gdn[...]
    saved.square_t[...] = (gdn * gdn).T.astype(BF16)


def back_mlp(grad, weights, saved, start):
    rows = slice(start, start + grad.shape[0])
    _, wproj, wup, wdown, gamma, _ = weights
    gdn = saved.gdn[rows, :]
    root = saved.root[rows, :]
    dpower = -0.5 * grad * gdn * (root * root * root)
    dpower_16 = dpower.astype(BF16)
    saved.dpower[rows, :] = dpower_16
    dgdn = grad * root + 2.0 * gdn * dot(dpower_16, gamma, (1, 1))
    dgdn_16 = dgdn.astype(BF16)
    saved.dgdn[rows, :] = dgdn_16
    dup = (dot(dgdn_16, wdown) * saved.slope[rows, :]).astype(BF16)
    saved.dup[rows, :] = dup
    dhidden = dgdn + norm_back(dot(dup, wup, (1, 1)), saved.hat2[rows, :], saved.scale2[rows, :])
    dhidden_16 = dhidden.astype(BF16)
    saved.dhidden[rows, :] = dhidden_16
    saved.dmixed[rows, :] = dot(dhidden_16, wproj, (1, 1)).astype(BF16)
    saved.wide[rows, :] = dhidden
    return jnp.sum(dpower, axis=0, keepdims=True)


def grads_mlp(saved, pack):
    down_grad = dot(saved.dgdn[...], saved.lifted[...], (0, 0))
    up_grad = dot(saved.hat2_t[...], saved.dup[...])
    gamma_grad = dot(saved.square_t[...], saved.dpower[...])
    for i in range(3):
        pack[C * i : C * (i + 1), :] = up_grad[:, 128 * i : 128 * (i + 1)].astype(BF16)
        pack[288 + C * i : 288 + C * (i + 1), :] = down_grad[:, 128 * i : 128 * (i + 1)].astype(BF16)
        pack[576 + C * i : 576 + C * (i + 1), C:128] = gamma_grad[:, 32 * i : 32 * (i + 1)].astype(BF16)
    pack[864:960, 0:C] = dot(saved.mixed_t[...], saved.dhidden[...]).astype(BF16)


def back_attention(saved):
    every = range(WINDOWS)
    dmixed = [stack_heads(window(saved.dmixed, w)) for w in every]
    dattns = [dot(window(saved.value, w), dmixed[w], (1, 1)) for w in every]
    dvalues = [dot(saved.attn[w].astype(BF16), dmixed[w]) for w in every]
    for w in every:
        put_window(saved.dvalue, w, dvalues[w])
    dscores = []
    for w in every:
        attn = saved.attn[w]
        dscores.append(attn * (dattns[w] - jnp.sum(attn * dattns[w], axis=0, keepdims=True)))
    total = dscores[0]
    for w in every[1:]:
        total = total + dscores[w]
    dscores = [(dscore * (HEAD**-0.5)).astype(BF16) for dscore in dscores]
    dqueries = [dot(dscores[w], window(saved.key, w), (0, 0)) for w in every]
    dkeys = [dot(dscores[w], stack_heads(window(saved.query, w))) for w in every]
    for w in every:
        put_window(saved.dkey, w, dkeys[w])
        put_window(saved.dquery, w, merge_heads(dqueries[w]))
    return total


def grads_attention(saved, pack, total, beta_grad, spread_ref):
    for i, part in enumerate((saved.dquery, saved.dkey, saved.dvalue)):
        pack[576 + C * i : 576 + C * (i + 1), 0:C] = dot(saved.normed_t[...], part[...]).astype(BF16)
    edge = jnp.concatenate([beta_grad, jnp.zeros((1, 128 - C), F32)], axis=1)
    lines = table_slots(total, spread_ref)
    rows = [edge] + [line[:, 128 * i : 128 * (i + 1)] for line in lines for i in range(2)]
    rows.append(jnp.zeros((ROWS - 967, 128), F32))
    pack[960:ROWS, :] = jnp.concatenate(rows, axis=0).astype(BF16)


def back_input(weights, saved):
    wq, wk, wv = weights[0]
    dnormed = dot(saved.dquery[...], wq, (1, 1)) + dot(saved.dkey[...], wk, (1, 1)) + dot(saved.dvalue[...], wv, (1, 1))
    return saved.wide[...] + norm_back(dnormed, saved.hat1[...], saved.scale1[...])


class Saved:
    names = {
        "hat1": ((PIX, C), F32),
        "scale1": ((PIX, 1), F32),
        "query": ((PIX, C), BF16),
        "key": ((PIX, C), BF16),
        "value": ((PIX, C), BF16),
        "bias": ((TOKENS, HEADS * TOKENS), F32),
        "attn": ((WINDOWS, TOKENS, HEADS * TOKENS), F32),
        "mixed": ((PIX, C), BF16),
        "hat2": ((PIX, C), F32),
        "scale2": ((PIX, 1), F32),
        "lifted": ((PIX, HID), BF16),
        "slope": ((PIX, HID), F32),
        "gdn": ((PIX, C), F32),
        "root": ((PIX, C), F32),
        "dmixed": ((PIX, C), BF16),
        "dquery": ((PIX, C), BF16),
        "dkey": ((PIX, C), BF16),
        "dvalue": ((PIX, C), BF16),
        "dpower": ((PIX, C), BF16),
        "dgdn": ((PIX, C), BF16),
        "dup": ((PIX, HID), BF16),
        "dhidden": ((PIX, C), BF16),
        "wide": ((PIX, C), F32),
        "normed_t": ((C, PIX), BF16),
        "hat2_t": ((C, PIX), BF16),
        "mixed_t": ((C, PIX), BF16),
        "square_t": ((C, PIX), BF16),
    }

    def __init__(self, refs):
        for name, ref in zip(Saved.names, refs):
            setattr(self, name, ref)


def copy_to(src, dst, send, recv, device):
    return pltpu.make_async_remote_copy(
        src_ref=src, dst_ref=dst, send_sem=send, recv_sem=recv, device_id=device, device_id_type=MESH
    )


def read_weights(b, refs):
    wqkv, wproj, wup, wdown, gamma, beta = refs
    whole = wqkv[b].astype(F32)
    parts = tuple(whole[:, C * i : C * (i + 1)].astype(BF16) for i in range(3))
    return parts, wproj[b], wup[b], wdown[b], gamma[b].astype(BF16), beta[b : b + 1, :]


class Exchange:
    width = QUAD
    turns = (2, 1, 3, 0)

    def __init__(self, n_lat, n_lon, base, pack, total, first, planes, mine, sems):
        self.n_lat, self.planes_n, self.size = n_lat, n_lon // QUAD, n_lat * self.width
        self.lat, self.lon = lax.axis_index("lat"), lax.axis_index("lon")
        self.z = self.lon // QUAD
        self.quad = self.column(self.lon)
        self.base, self.pack, self.total = base, pack, total
        self.first, self.planes, self.mine, self.sems = first, planes, mine, sems
        self.rows = first.shape[1]
        self.place = self.lat * self.width + self.quad

    def column(self, lon):
        return lax.rem(lon, QUAD)

    def device_of(self, lat, quad):
        return (lat, self.z * QUAD + quad)

    def piece(self, ref, i):
        return ref.at[pl.ds(pl.multiple_of(self.base + i * self.rows, UNIT), self.rows), :]

    def in_plane(self, make):
        for i in range(self.n_lat - 1):
            step = (4 * i + 1) % 7 + 1 if self.n_lat == 8 else i + 1
            for turn in self.turns:
                make(step, turn).start()
        for turn in self.turns[:-1]:
            make(0, turn).start()

    def target(self, step, turn):
        lat = lax.rem(self.lat + step, self.n_lat)
        quad = lax.rem(self.quad + turn, self.width)
        return lat * self.width + quad, self.device_of(lat, quad)

    def scatter_copy(self, step, turn):
        place, device = self.target(step, turn)
        slot = self.first.at[step * self.width + turn]
        return copy_to(self.piece(self.pack, place), slot, self.sems.at[0], self.sems.at[1], device)

    def gather_copy(self, step, turn):
        _, device = self.target(step, turn)
        return copy_to(self.mine, self.piece(self.total, self.place), self.sems.at[4], self.sems.at[5], device)

    def own_copy(self):
        return pltpu.make_async_copy(self.mine, self.piece(self.total, self.place), self.sems.at[6])

    def plane_copy(self, step):
        slot = self.planes.at[self.z]
        device = (self.lat, lax.rem(self.lon + step * QUAD, self.planes_n * QUAD))
        return copy_to(slot, slot, self.sems.at[2], self.sems.at[3], device)

    def wait_both(self, ref, sem):
        for i in range(2):
            pltpu.make_async_copy(ref, ref, self.sems.at[sem + i]).wait()

    def start(self):
        self.in_plane(self.scatter_copy)

    def add_plane(self):
        self.wait_both(self.first.at[pl.ds(1, self.size - 1)], 0)
        total = self.piece(self.pack, self.place)[...].astype(F32)
        for i in range(1, self.size):
            total = total + self.first[i].astype(F32)
        self.planes[self.z] = total.astype(BF16)

        def body(step, _):
            self.plane_copy(step).start()
            return 0

        lax.fori_loop(1, self.planes_n, body, 0)

    def add_all(self, factor):
        if self.planes_n > 1:
            self.wait_both(self.planes.at[pl.ds(0, self.planes_n - 1)], 2)
        total = self.planes[0].astype(F32)
        for i in range(1, self.planes_n):
            total = total + self.planes[i].astype(F32)
        self.mine[...] = (total * factor).astype(BF16)
        self.in_plane(self.gather_copy)
        self.own_copy().start()

    def finish(self):
        self.wait_both(self.total.at[pl.ds(0, (self.size - 1) * self.rows), :], 4)
        self.own_copy().wait()


class PairedExchange(Exchange):
    width = QUAD // 2
    turns = (1, 0)

    def __init__(self, n_lat, n_lon, pack, total, half, first, planes, mine, sems):
        self.half = half
        self.core = lax.rem(lax.axis_index("lon"), 2)
        super().__init__(n_lat, n_lon, self.core * (ROWS // 2), pack, total, first, planes, mine, sems)

    def column(self, lon):
        return lax.rem(lon, QUAD) // 2

    def device_of(self, lat, quad):
        return (lat, self.z * QUAD + quad * 2 + self.core)

    def half_of(self, ref, core):
        return ref.at[pl.ds(pl.multiple_of(core * (ROWS // 2), ROWS // 2), ROWS // 2), :]

    def pair_copy(self):
        device = (self.lat, self.lon + 1 - 2 * self.core)
        return copy_to(self.half_of(self.pack, 1 - self.core), self.half, self.sems.at[7], self.sems.at[8], device)

    def swap_copy(self):
        device = (self.lat, self.lon + 1 - 2 * self.core)
        mine = self.half_of(self.total, self.core)
        return copy_to(mine, mine, self.sems.at[9], self.sems.at[10], device)

    def start_pair(self):
        self.pair_copy().start()

    def add_pair(self):
        self.pair_copy().wait()
        mine = self.half_of(self.pack, self.core)
        mine[...] = (mine[...].astype(F32) + self.half[...].astype(F32)).astype(BF16)
        self.start()

    def swap(self):
        super().finish()
        self.swap_copy().start()

    def finish(self):
        self.swap_copy().wait()


def exchange_scratch(n_lat, n_lon, rows, members):
    rows = rows // members
    return [
        pltpu.VMEM((members, rows, 128), BF16),
        pltpu.VMEM((n_lon // QUAD, rows, 128), BF16),
        pltpu.VMEM((rows, 128), BF16),
        pltpu.SemaphoreType.DMA((11,)),
    ]


def unpack(b, total, outs):
    qkv, proj, up, down, gamma, beta, table = outs
    first = total[576:864, :].astype(F32)
    parts = [first[C * i : C * (i + 1)] for i in range(3)]
    qkv[b] = jnp.concatenate([part[:, 0:C] for part in parts], axis=1)
    gamma[b] = jnp.concatenate([part[:, C:128] for part in parts], axis=1)
    proj[b] = total[864:960, 0:C].astype(F32)
    for i in range(3):
        up[b, :, 128 * i : 128 * (i + 1)] = total[C * i : C * (i + 1), :].astype(F32)
        down[b, :, 128 * i : 128 * (i + 1)] = total[288 + C * i : 288 + C * (i + 1), :].astype(F32)
    edge = total[960:976, :].astype(F32)
    beta[b : b + 1, :] = edge[0:1, 0:C]
    lines = [jnp.concatenate([edge[1 + 2 * h : 2 + 2 * h], edge[2 + 2 * h : 3 + 2 * h]], axis=1) for h in range(HEADS)]
    slots = jnp.concatenate(lines, axis=0).astype(BF16)
    table[:, b, :] = dot(slots, rel_slots().astype(BF16), (1, 1))


def unpack_kernel(*refs):
    ins, outs, staged, held, sems = refs[:4], refs[4:13], refs[13:20], refs[20:24], refs[24]
    loads = [pltpu.make_async_copy(src, dst, sems.at[i]) for i, (src, dst) in enumerate(zip(ins, held))]
    for i in (3, 2, 0, 1):
        loads[i].start()
    copies = []

    def store(src, dst):
        copies.append(pltpu.make_async_copy(src, dst, sems.at[4 + len(copies)]))
        copies[-1].start()

    for b in (1, 0):
        loads[2 + b].wait()
        unpack(b, held[2 + b], staged)
        for src, dst in zip(staged[:5], outs[2:7]):
            store(src.at[b], dst.at[b])
        loads[b].wait()
        store(held[b], outs[b])
    for src, dst in zip(staged[5:], outs[7:]):
        store(src, dst)
    for copy in copies:
        copy.wait()


def kernel(n_lat, n_lon, *refs):
    refs = list(refs)

    def take(count):
        taken = refs[:count]
        del refs[:count]
        return taken

    hbm_args = take(9)
    results = take(4)
    args = take(9)
    arg_sems, slot_ref, spread_ref = take(3)
    saved = [Saved(take(len(Saved.names))) for _ in range(2)]
    field, send_out, send_cot, send_dec, send_grad = take(5)
    south, east, corner, halo_send, halo_recv = take(5)
    packs, fields = take(2), take(2)
    (staged,) = take(1)
    (result_sems,) = take(1)
    whole = PairedExchange(n_lat, n_lon, packs[1], staged, *take(5))
    upper = Exchange(n_lat, n_lon, 0, packs[0], results[2], *take(4))
    lower = Exchange(n_lat, n_lon, ROWS // 2, packs[0], results[2], *take(4))
    lat, lon = lax.axis_index("lat"), lax.axis_index("lon")
    above, below = lax.rem(lat + n_lat - 1, n_lat), lax.rem(lat + 1, n_lat)
    west, easterly = lax.rem(lon + n_lon - 1, n_lon), lax.rem(lon + 1, n_lon)

    stores = [
        pltpu.make_async_copy(src, dst, result_sems.at[i]) for i, (src, dst) in enumerate(zip(fields + [staged], results[:2] + results[3:]))
    ]
    loads = [pltpu.make_async_copy(src, dst, arg_sems.at[i]) for i, (src, dst) in enumerate(zip(hbm_args, args))]
    for load in loads:
        load.start()
    barrier = pltpu.get_barrier_semaphore()

    def greet(device):
        pl.semaphore_signal(barrier, inc=1, device_id=device, device_id_type=MESH)

    def greet_plane(i, _):
        _, device = upper.target(i // QUAD, lax.rem(i, QUAD))
        greet(device)
        return 0

    def greet_planes(i, _):
        greet((lat, lax.rem(lon + QUAD * i, n_lon)))
        return 0

    planes_n = n_lon // QUAD
    lax.fori_loop(1, n_lat * QUAD, greet_plane, 0)
    lax.fori_loop(1, planes_n, greet_planes, 0)
    for device in ((lat, west), (lat, easterly), (above, west), (below, easterly)):
        greet(device)
    greetings = n_lat * QUAD + planes_n + 2

    def halo(i, ref, rows, devices):
        copies = []
        for j, target in enumerate((south, east, corner)):
            src = ref.at[pl.ds(rows[j][0], rows[j][1]), :]
            k = 3 * i + j
            copies.append(copy_to(src, target.at[i], halo_send.at[k], halo_recv.at[k], devices[j]))
        return copies

    def up_halo(i, ref):
        rows = ((0, HALF), (HALF, UNIT), (0, UNIT))
        return halo(i, ref, rows, ((above, lon), (lat, west), (above, west)))

    def down_halo(i, ref):
        rows = ((HALF, HALF), (HALF - UNIT, UNIT), (PIX - UNIT, UNIT))
        return halo(i, ref, rows, ((below, lon), (lat, easterly), (below, easterly)))

    def shifted(i, ref):
        parts = [ref[HALF + UNIT : PIX, :], east[i], south[i, UNIT:HALF, :], corner[i]]
        return jnp.concatenate([part.astype(F32) for part in parts], axis=0)

    def unshifted(i, ref):
        parts = [corner[i], south[i, 0 : HALF - UNIT, :], east[i], ref[0 : HALF - UNIT, :]]
        return jnp.concatenate([part.astype(F32) for part in parts], axis=0)

    sig, cot, table = args[0], args[1], args[8]
    slot_ref[...] = rel_slots().astype(BF16)
    spread_ref[...] = spread_queries().astype(BF16)
    loads[8].wait()
    build_bias(table[:, 0, :], slot_ref, spread_ref, saved[0].bias)
    for load in loads[:8]:
        load.wait()
    unfold(sig, field)
    weights = [read_weights(0, args[2:8])]
    project(field[...], weights[0], saved[0], 0)
    output = forward(field[...], weights[0], saved[0], None, True)
    send_out[...] = output.astype(BF16)

    pl.semaphore_wait(barrier, greetings)
    out_copies = up_halo(0, send_out)
    for copy in out_copies:
        copy.start()
    unfold(cot, send_cot)
    cot_copies = up_halo(1, send_cot)
    for copy in cot_copies:
        copy.start()
    build_bias(table[:, 1, :], slot_ref, spread_ref, saved[1].bias)
    is_last = (lat == n_lat - 1).astype(jnp.int32)
    shape = (TOKENS, HEADS * TOKENS)
    differ = (iota(shape, 0) // 32 != (iota(shape, 1) % TOKENS) // 32).astype(jnp.int32)
    blocked = differ * is_last > 0
    weights.append(read_weights(1, args[2:8]))
    own = HALF - UNIT
    project(send_out[HALF + UNIT : PIX, :].astype(F32), weights[1], saved[1], 0)
    prepare(saved[0])
    for copy in out_copies:
        copy.wait()
    field[...] = shifted(0, send_out)
    project(field[own:PIX, :], weights[1], saved[1], own)
    output = forward(field[...], weights[1], saved[1], blocked, False)
    send_dec[...] = output.astype(BF16)
    dec_copies = down_halo(2, send_dec)
    for copy in dec_copies:
        copy.start()
    for copy in cot_copies:
        copy.wait()
    beta_grad = back_mlp(shifted(1, send_cot), weights[1], saved[1], 0)
    total = back_attention(saved[1])
    send_grad[...] = back_input(weights[1], saved[1]).astype(BF16)
    grad_copies = down_halo(3, send_grad)
    for copy in grad_copies:
        copy.start()
    transpose_saved(saved[1])
    grads_mlp(saved[1], packs[1])
    grads_attention(saved[1], packs[1], total, beta_grad, spread_ref)
    whole.start_pair()
    for copy in dec_copies:
        copy.wait()
    fold(unshifted(2, send_dec), fields[0])
    stores[0].start()
    transpose_saved(saved[0])
    beta_grad = back_mlp(send_grad[0:own, :].astype(F32), weights[0], saved[0], PIX - own)
    whole.add_pair()
    for copy in grad_copies:
        copy.wait()
    factor = 1.0 / math.sqrt(PIX * n_lat * n_lon)

    field[...] = unshifted(3, send_grad)
    beta_grad = beta_grad + back_mlp(field[0 : PIX - own, :], weights[0], saved[0], 0)
    grads_mlp(saved[0], packs[0])
    upper.start()
    total = back_attention(saved[0])
    grads_attention(saved[0], packs[0], total, beta_grad, spread_ref)
    lower.start()
    fold(back_input(weights[0], saved[0]), fields[1])
    stores[1].start()
    whole.add_plane()
    upper.add_plane()
    lower.add_plane()
    whole.add_all(factor)
    upper.add_all(factor)
    lower.add_all(factor)
    whole.swap()
    upper.finish()
    whole.finish()
    stores[2].start()
    lower.finish()
    for store in stores:
        store.wait()


def solution(mesh):
    n_lat, n_lon = mesh.shape["lat"], mesh.shape["lon"]

    def per_device(sig, cot, wqkv, wproj, wup, wdown, gamma, beta, table):
        dma = pltpu.SemaphoreType.DMA
        args = (sig, cot, wqkv, wproj, wup, jnp.swapaxes(wdown, 1, 2), gamma, beta, jnp.swapaxes(table, 0, 1))
        saved = [pltpu.VMEM(shape, kind) for shape, kind in Saved.names.values()]
        scratch = [pltpu.VMEM(arg.shape, arg.dtype) for arg in args] + [dma((9,))]
        scratch += [pltpu.VMEM((RELS, SLOTS), BF16), pltpu.VMEM((HEADS * TOKENS, HEADS * 128), BF16)]
        scratch += saved + saved
        scratch += [pltpu.VMEM((PIX, C), F32)] + [pltpu.VMEM((PIX, C), BF16)] * 4
        scratch += [
            pltpu.VMEM((4, HALF, C), BF16),
            pltpu.VMEM((4, UNIT, C), BF16),
            pltpu.VMEM((4, UNIT, C), BF16),
            dma((12,)),
            dma((12,)),
        ]
        scratch += [pltpu.VMEM((ROWS, 128), BF16)] * 2 + [pltpu.VMEM(sig.shape, BF16)] * 2
        scratch += [pltpu.VMEM((ROWS, 128), BF16), dma((3,))]
        scratch += [pltpu.VMEM((ROWS // 2, 128), BF16)]
        scratch += exchange_scratch(n_lat, n_lon, ROWS // 2, n_lat * QUAD // 2)
        scratch += exchange_scratch(n_lat, n_lon, ROWS // 2, n_lat * QUAD) * 2
        hbm = pl.BlockSpec(memory_space=pltpu.HBM)
        field = jax.ShapeDtypeStruct(sig.shape, BF16)
        total = jax.ShapeDtypeStruct((ROWS, 128), BF16)
        results = pl.pallas_call(
            functools.partial(kernel, n_lat, n_lon),
            out_shape=[field, field, total, total],
            in_specs=[hbm] * 9,
            out_specs=[hbm] * 4,
            scratch_shapes=scratch,
            compiler_params=pltpu.CompilerParams(
                collective_id=0, has_side_effects=True, vmem_limit_bytes=62 * 1024 * 1024
            ),
        )(*args)
        grads = [jax.ShapeDtypeStruct(leaf.shape, F32) for leaf in args[2:]]
        outs = pl.pallas_call(
            unpack_kernel,
            out_shape=[field, field] + grads,
            in_specs=[hbm] * 4,
            out_specs=[hbm] * 9,
            scratch_shapes=[pltpu.VMEM(leaf.shape, F32) for leaf in args[2:]]
            + [pltpu.VMEM(sig.shape, BF16)] * 2
            + [pltpu.VMEM((ROWS, 128), BF16)] * 2
            + [dma((18,))],
            compiler_params=pltpu.CompilerParams(vmem_limit_bytes=62 * 1024 * 1024),
        )(*results)
        decoded, sgrad, qkv, proj, up, down, gammas, betas, tables = outs
        return decoded, sgrad, qkv, proj, up, jnp.swapaxes(down, 1, 2), gammas, betas, jnp.swapaxes(tables, 0, 1)

    in_specs = (P("lat", "lon"), P("lat", "lon"), P(), P(), P(), P(), P(), P(), P())
    out_specs = (P("lat", "lon"), P("lat", "lon"), P(), P(), P(), P(), P(), P(), P())
    return jax.shard_map(per_device, mesh=mesh, in_specs=in_specs, out_specs=out_specs, check_vma=False)
```
